32 devices in a mesh: dom: 4 (over z), sub: 8 (over y, x, core).
Axes of the slice: x: 2, y: 2, z: 4, core: 2. Of those that a mesh axis runs over, the one named last changes fastest.
Arguments:
- blocks: bfloat16 [7168, 128, 128], P(('dom', 'sub')), may hold values from -0.1875 to 0.1875
- vectors: bfloat16 [16, 131072], P(None, ('dom', 'sub')), may hold values from -205 to 205, as said below
- col_index: int32 [32, 224], P(('dom', 'sub')), may hold values from 0 to 47, as said below
- row_ptr: int32 [32, 33], P(('dom', 'sub')), may hold values from 0 to 224, as said below
- send_list: int32 [32, 8, 2], P(('dom', 'sub')), may hold values from 0 to 31
Outputs:
- new_basis: float32 [16, 131072], P(None, ('dom', 'sub'))
- upper_factor: float32 [16, 16], replicated
- gain: float32 [16], replicated
The draws below stay inside these ranges and needn't reach their ends.
Inputs may be any that keep to these rules, and one draw needn't show every extreme that they name: `col_index`: every stored block row holds 5 or 9 blocks, half of each device's rows 9. Its first three columns are its own row, the next and the previous own row (cyclically within the device); the rest are distinct ghost slots, and every ghost slot of every device is used by some block. `row_ptr`: each device's row pointers start at 0, rise by 5 or 9, and end at 224. `vectors`: rows and columns have unlike scales.
All inputs are finite; a program needn't handle non-finite values.
Results may differ from the reference program's by a relative error of at most 0.0028.
Values may be sent and summed in bfloat16 or wider, within the bound.
No kernel may reach another device: no remote copies, remote signals or barrier semaphores. Data moves between devices by JAX's collectives and lax.ppermute only.
A program may use at most 64 MiB of HBM per device.

```python
import math
import jax
import jax.numpy as jnp
from jax import lax

B = 128
K = 16
RB_DEV = 32
NEIGHBOURS = 8
GHOST = 2
NNZ_DEV = 224
SLOTS = 16
ROWS = 131072
N_SUB = 8
DEVICES = 32


def pattern(key):
    key_list = jax.random.split(jax.random.fold_in(key, 17), DEVICES)

    def per_device(device_key):
        first_key, second_key = jax.random.split(device_key)
        row_order = jax.random.permutation(first_key, RB_DEV).astype(jnp.int32)
        lengths = 5 + 4 * (row_order < RB_DEV // 2).astype(jnp.int32)
        starts = jnp.concatenate([jnp.zeros((1,), jnp.int32), jnp.cumsum(lengths).astype(jnp.int32)])
        entries = jnp.arange(NNZ_DEV, dtype=jnp.int32)
        row_of = jnp.sum((starts[1:-1][None, :] <= entries[:, None]).astype(jnp.int32), axis=1).astype(jnp.int32)
        within = entries - starts[row_of]
        slot_order = jax.random.permutation(second_key, SLOTS).astype(jnp.int32)
        ghost_count = entries - 3 * row_of - 3
        ghost_cols = RB_DEV + slot_order[jnp.mod(ghost_count, SLOTS)]
        local_cols = jnp.where(within == 0, row_of, jnp.where(within == 1, jnp.mod(row_of + 1, RB_DEV), jnp.mod(row_of + RB_DEV - 1, RB_DEV)))
        columns = jnp.where(within < 3, local_cols, ghost_cols).astype(jnp.int32)
        return (columns, starts)
    return jax.vmap(per_device)(key_list)


def draw_col_index(key, part):
    return pattern(key)[0]


def draw_row_ptr(key, part):
    return pattern(key)[1]


def draw_vectors(key, part):
    first_key, second_key, third_key = jax.random.split(jax.random.fold_in(key, 5), 3)
    block_count = ROWS // B
    random_part = jnp.clip(jax.random.normal(first_key, (K, ROWS), jnp.float32), -4.0, 4.0)
    row_scale = jnp.exp(jax.random.uniform(second_key, (block_count,), jnp.float32) * math.log(10.0))
    row_trend = 1.0 + 2.0 * jnp.arange(ROWS, dtype=jnp.float32) / ROWS
    col_scale = jnp.exp(jax.random.uniform(third_key, (K, 1), jnp.float32) * math.log(10.0))
    values = 0.1 * random_part * col_scale * jnp.repeat(row_scale, B)[None, :] * row_trend[None, :]
    return values.astype(jnp.bfloat16)


def place_ends(values, own_key, low, largest):
    dims = values.shape
    index_at = [jax.random.randint(jax.random.fold_in(own_key, axis), (), 0, dims[axis]) for axis in range(len(dims))]
    values = values.at[tuple(index_at)].set(low)
    longest = dims.index(max(dims))
    index_at[longest] = (index_at[longest] + 1) % dims[longest]
    return values.at[tuple(index_at)].set(largest)


def steps_of(stream_key, extent, shards, low, largest):
    level = 1.0
    for dim, blocks in shards:
        draws = jax.random.uniform(jax.random.fold_in(jax.random.fold_in(stream_key, 6), dim), (blocks,), jnp.float32, low / len(shards), largest / len(shards))
        level = level * jnp.repeat(jnp.exp(draws), extent[dim] // blocks).reshape((-1,) + (1,) * (len(extent) - 1 - dim))
    return level


def bell_draw(own_key, extent, width, reach, shards=(), kind=jnp.bfloat16):
    values = width * jax.random.normal(own_key, extent, jnp.float32)
    if shards:
        values = values * steps_of(own_key, extent, shards, -0.22, 0.18)
    return jnp.clip(values, -reach, reach).astype(kind)


def setup_inputs(seed: int = 0) -> dict:
    key_of = jax.random.split(jax.random.key(seed), 6)
    return {
        "blocks": bell_draw(key_of[0], (DEVICES * NNZ_DEV, B, B), (7 * B) ** -0.5, 0.1875, ((0, 32),)),
        "vectors": draw_vectors(jax.random.fold_in(key_of[5], 71), 0),
        "col_index": draw_col_index(jax.random.fold_in(key_of[5], 71), 0),
        "row_ptr": draw_row_ptr(jax.random.fold_in(key_of[5], 71), 0),
        "send_list": place_ends(jax.random.randint(key_of[4], (DEVICES, NEIGHBOURS, GHOST), 0, RB_DEV), jax.random.fold_in(key_of[4], 1), 0, RB_DEV - 1).astype(jnp.int32),
    }


def reference(blocks, vectors, col_index, row_ptr, send_list):
    stacked = blocks.reshape(DEVICES, NNZ_DEV, B, B)
    whole_v = vectors.reshape(K, DEVICES * RB_DEV, B)
    entries = jnp.arange(NNZ_DEV, dtype=jnp.int32)
    combined_ids = jnp.arange(RB_DEV + SLOTS, dtype=jnp.int32)
    offset_table = jnp.array([outer_step * N_SUB + inner_step for outer_step in (-1, 0, 1) for inner_step in (-1, 0, 1) if outer_step != 0 or inner_step != 0], dtype=jnp.int32)

    def resolve(device, columns):
        shifted = jnp.maximum(columns - RB_DEV, 0).astype(jnp.int32)
        neighbour = shifted // GHOST
        source = jnp.mod(device - offset_table[neighbour] + DEVICES, DEVICES).astype(jnp.int32)
        ghost_rows = source * RB_DEV + send_list[source, neighbour, shifted % GHOST]
        return jnp.where(columns < RB_DEV, device * RB_DEV + columns, ghost_rows).astype(jnp.int32)

    def row_numbers(device):
        starts = row_ptr[device]
        return jnp.sum((starts[1:-1][None, :] <= entries[:, None]).astype(jnp.int32), axis=1).astype(jnp.int32)

    def forward(device):
        targets = resolve(device, col_index[device].astype(jnp.int32))
        row_of = row_numbers(device)
        picked = whole_v[:, targets, :].astype(jnp.float32)
        products = jnp.einsum('kne,nce->knc', picked, stacked[device].astype(jnp.float32))
        summed = jax.ops.segment_sum(jnp.transpose(products, (1, 0, 2)), row_of, num_segments=RB_DEV)
        return jnp.transpose(summed, (1, 0, 2)).astype(jnp.bfloat16)
    device_ids = jnp.arange(DEVICES, dtype=jnp.int32)
    pieces = lax.map(forward, device_ids)
    image_rows = jnp.transpose(pieces, (1, 0, 2, 3)).reshape(K, DEVICES * RB_DEV, B)
    image_rows = lax.optimization_barrier(image_rows)
    gain = jnp.sum(jnp.square(image_rows.astype(jnp.float32)), axis=(1, 2)) / ROWS

    def backward(device):
        columns = col_index[device].astype(jnp.int32)
        row_of = row_numbers(device)
        rows_here = image_rows[:, device * RB_DEV + row_of, :].astype(jnp.float32)
        partial_terms = jnp.einsum('knc,ncb->nkb', rows_here, stacked[device].astype(jnp.float32))
        local_sums = jax.ops.segment_sum(partial_terms, columns, num_segments=RB_DEV + SLOTS)
        return (local_sums, resolve(device, combined_ids))
    local_all, target_all = lax.map(backward, device_ids)
    flat_terms = local_all.reshape(DEVICES * (RB_DEV + SLOTS), K, B)
    owned = jax.ops.segment_sum(flat_terms, target_all.reshape(-1), num_segments=DEVICES * RB_DEV)
    flat = jnp.transpose(owned, (1, 0, 2)).reshape(K, ROWS)
    gram = jnp.dot(flat, flat.T, precision=lax.Precision.HIGHEST) / ROWS
    lower_factor = jnp.linalg.cholesky(gram)
    new_basis = lax.linalg.triangular_solve(lower_factor, flat, left_side=True, lower=True)
    return (new_basis, lower_factor.T, gain)
```

```python
import functools

import jax
import jax.numpy as jnp
from jax import lax
from jax.experimental import pallas as pl
from jax.experimental.pallas import tpu as pltpu
from jax.sharding import PartitionSpec as P

AXES = ("dom", "sub")
B = 128
SHORT = 5
LONG = 9
LOCAL = 3
F32 = jnp.float32
BF16 = jnp.bfloat16
BY_LAST = (((1,), (1,)), ((), ()))
BY_FIRST = (((1,), (0,)), ((), ()))
VMEM = pl.BlockSpec(memory_space=pltpu.VMEM)
SMEM = pl.BlockSpec(memory_space=pltpu.SMEM)
LIMIT = 40 * 2**20


def neighbour(a, b):
    place = (a + 1) * 3 + b + 1
    return place - (place > 4)


def outward():
    return 2 * lax.rem(lax.axis_index("sub"), 2) - 1


def columns(block_row):
    return pl.ds(pl.multiple_of(block_row * B, B), B)


def joined(ref, places, axis):
    return jnp.concatenate([ref[place] for place in places], axis=axis)


def sent(s):
    return (
        ((0, -s), (1, -s), (-1, -s)),
        ((0, s),),
        ((s, s),),
        ((-s, s),),
        ((1, 0),),
        ((-1, 0),),
    )


def received(s):
    return (
        ((0, s),),
        ((0, -s),),
        ((-s, -s),),
        ((s, -s),),
        ((1, 0), (1, s)),
        ((-1, 0), (-1, s)),
    )


def exchange(pair, side, outer, inner, up, down):
    n_inner = lax.axis_size("sub")
    devices = lax.axis_size("dom") * n_inner

    def move(array, odd, even):
        return lax.ppermute(
            array,
            AXES,
            [(d, (d + (odd if d % 2 else even)) % devices) for d in range(devices)],
        )

    pair = move(pair, -1, 1)
    side = move(side, 1, -1)
    outer = move(outer, n_inner + 1, -n_inner - 1)
    inner = move(inner, 1 - n_inner, n_inner - 1)
    up = move(jnp.concatenate([up, pair[1:2]], axis=0), n_inner, n_inner)
    down = move(jnp.concatenate([down, pair[2:3]], axis=0), -n_inner, -n_inner)
    return pair, side, outer, inner, up, down


def gather_kernel(send, vectors, *outgoing):
    for ref, offsets in zip(outgoing, sent(outward())):
        for i, (a, b) in enumerate(offsets):
            for g in range(send.shape[2]):
                ref[i, g] = vectors[:, columns(send[0, neighbour(a, b), g])]


def local_forward_kernel(ptr, vectors, blocks, image):
    rows = image.shape[0]
    for j in range(rows):
        e = ptr[0, j]
        near = [vectors[:, c * B : c * B + B] for c in (j, (j + 1) % rows, (j - 1) % rows)]
        image[j] = lax.dot_general(
            jnp.concatenate(near, axis=1),
            joined(blocks, [e + t for t in range(LOCAL)], 1),
            BY_LAST,
            preferred_element_type=F32,
        )


def ghost_kernel(ptr, col, blocks, partial_image, *refs):
    arrived, image, outgoing = refs[:6], refs[6], refs[7:13]
    ghosts, total, spread, long_rows = refs[13:]
    rows = image.shape[0]
    many = long_rows.shape[0] - 1
    s = outward()
    for ref, offsets in zip(arrived, received(s)):
        for i, (a, b) in enumerate(offsets):
            for g in range(ref.shape[1]):
                ghosts[neighbour(a, b) * ref.shape[1] + g] = ref[i, g]
    found = 0
    for j in range(rows):
        long_rows[jnp.minimum(found, many)] = j
        found = found + (ptr[0, j + 1] - ptr[0, j] > SHORT).astype(jnp.int32)

    def forward(e, first, last):
        return lax.dot_general(
            joined(ghosts, [col[0, e + t] - rows for t in range(first, last)], 1),
            joined(blocks, [e + t for t in range(first, last)], 1),
            BY_LAST,
            preferred_element_type=F32,
        )

    for j in range(rows):
        total[j] = partial_image[j] + forward(ptr[0, j], LOCAL, SHORT)
    for i in range(many):
        j = long_rows[i]
        total[j] += forward(ptr[0, j], SHORT, LONG)
    image[...] = total[...].astype(BF16)
    spread[...] = jnp.zeros_like(spread)
    banks = spread.shape[0]

    def backward(j, first, last):
        e = ptr[0, j]
        terms = lax.dot_general(
            image[j],
            joined(blocks, [e + t for t in range(first, last)], 1),
            BY_FIRST,
            preferred_element_type=F32,
        )
        for t in range(first, last):
            k = t - first
            spread[k % banks, col[0, e + t] - rows] += terms[:, k * B : k * B + B]

    for j in range(rows):
        backward(j, LOCAL, SHORT)
    for i in range(many):
        backward(long_rows[i], SHORT, LONG)
    for ref, offsets in zip(outgoing, sent(s)):
        for i, (a, b) in enumerate(offsets):
            for g in range(ref.shape[1]):
                slot = neighbour(-a, -b) * ref.shape[1] + g
                ref[i, g] = sum(spread[bank, slot] for bank in range(banks))


def local_backward_kernel(ptr, blocks, image, adjoint, squares):
    rows = image.shape[0]
    total = jnp.zeros(squares.shape, F32)
    for j in range(rows):
        before, after = (j - 1) % rows, (j + 1) % rows
        adjoint[:, j * B : j * B + B] = lax.dot_general(
            joined(image, [j, before, after], 1),
            joined(blocks, [ptr[0, j], ptr[0, before] + 1, ptr[0, after] + 2], 0),
            BY_FIRST,
            preferred_element_type=F32,
        )
        wide = image[j].astype(F32)
        total = total + wide * wide
    squares[...] = total


def group_masks(k):
    group = B // k
    row = lax.broadcasted_iota(jnp.int32, (k, B), 0)
    lane = lax.broadcasted_iota(jnp.int32, (k, B), 1)
    return lax.rem(row, group) == lax.div(lane, k), row, lane


def gram_kernel(send, partial_adjoint, squares, *refs):
    arrived, adjoint, packed = refs[:6], refs[6], refs[7]
    k = adjoint.shape[0]
    s = outward()
    adjoint[...] = partial_adjoint[...]
    for ref, offsets in zip(arrived, received(s)):
        for i, (a, b) in enumerate(offsets):
            for g in range(ref.shape[1]):
                place = columns(send[0, neighbour(-a, -b), g])
                adjoint[:, place] += ref[i, g]
    z = adjoint[...]
    gram = lax.dot_general(z, z, BY_LAST, precision=lax.Precision.HIGHEST, preferred_element_type=F32)
    own, row, lane = group_masks(k)
    tile = (lax.rem(lane, k) == row).astype(F32)
    tiled = lax.dot_general(gram, tile, BY_FIRST, precision=lax.Precision.HIGHEST, preferred_element_type=F32)
    tiled = jnp.where(own, tiled, 0.0)
    group = B // k
    lines = [jnp.sum(tiled[i : i + group], axis=0, keepdims=True) for i in range(0, k, group)]
    norms = jnp.sum(squares[...], axis=1, keepdims=True)
    lines.append(jnp.sum(jnp.where(lane == row, norms, 0.0), axis=0, keepdims=True))
    lines.append(jnp.zeros(((-len(lines)) % 4, B), F32))
    packed[...] = jnp.broadcast_to(jnp.concatenate(lines, axis=0)[None], packed.shape)


def solve_kernel(count, packed, adjoint, basis, factor, gain):
    k = adjoint.shape[0]
    group = B // k
    own, row, lane = group_masks(k)
    sums = jnp.sum(packed[...], axis=0) / count
    spread = jnp.concatenate(
        [jnp.broadcast_to(sums[i : i + 1], (group, B)) for i in range(k // group)], axis=0
    )
    line = lax.broadcasted_iota(jnp.int32, (B, B), 0)
    column = lax.broadcasted_iota(jnp.int32, (B, B), 1)
    fold = (lax.rem(line, k) == column).astype(F32)
    both = lax.dot_general(
        jnp.where(own, spread, 0.0), fold, BY_FIRST, precision=lax.Precision.HIGHEST, preferred_element_type=F32
    )
    both = both + (lane == row + k).astype(F32)
    for i in range(k):
        pivots = jnp.broadcast_to(both[:, i : i + 1], (k, B))
        scale = lax.rsqrt(pivots[i : i + 1])
        top = both[i : i + 1] * scale
        lower = both - pivots * scale * top
        both = jnp.where(row > i, lower, jnp.where(row == i, top, both))
    factor[...] = jnp.where(lane >= row, both, 0.0)[:, :k]
    gain[...] = sums[k // group : k // group + 1, :k]
    inverse = both[:, k : 2 * k]
    basis[...] = lax.dot_general(
        inverse, adjoint[...], BY_FIRST, precision=lax.Precision.HIGHEST, preferred_element_type=F32
    )


def call(kernel, name, shapes, in_specs, scratch=(), flops=0, bytes_accessed=0):
    return pl.pallas_call(
        kernel,
        name=name,
        out_shape=[jax.ShapeDtypeStruct(shape, dtype) for shape, dtype in shapes],
        in_specs=in_specs,
        out_specs=[VMEM] * len(shapes),
        scratch_shapes=scratch,
        compiler_params=pltpu.CompilerParams(vmem_limit_bytes=LIMIT),
        cost_estimate=pl.CostEstimate(flops=flops, bytes_accessed=bytes_accessed, transcendentals=0),
    )


def local(blocks, vectors, col_index, row_ptr, send_list):
    k, unknowns = vectors.shape
    rows = unknowns // B
    stored = blocks.shape[0]
    devices = lax.axis_size("dom") * lax.axis_size("sub")
    ghost = send_list.shape[2]
    slots = send_list.shape[1] * ghost
    many = (stored - SHORT * rows) // (LONG - SHORT)
    sizes = (3, 1, 1, 1, 1, 1)
    held = pltpu.with_memory_space_constraint(blocks, pltpu.VMEM)
    outgoing = call(
        gather_kernel,
        "gather",
        [((n, ghost, k, B), BF16) for n in sizes],
        [SMEM, VMEM],
    )(send_list, vectors)
    arrived = exchange(*outgoing)
    (partial_image,) = call(
        local_forward_kernel,
        "local_forward",
        [((rows, k, B), F32)],
        [SMEM, VMEM, VMEM],
        flops=2 * rows * LOCAL * B * B * k,
        bytes_accessed=2 * rows * LOCAL * B * B,
    )(row_ptr, vectors, held)
    image, *returns = call(
        ghost_kernel,
        "ghost",
        [((rows, k, B), BF16)] + [((n, ghost, k, B), F32) for n in sizes],
        [SMEM, SMEM] + [VMEM] * 8,
        scratch=[
            pltpu.VMEM((slots, k, B), BF16),
            pltpu.VMEM((rows, k, B), F32),
            pltpu.VMEM((4, slots, k, B), F32),
            pltpu.SMEM((many + 1,), jnp.int32),
        ],
        flops=4 * (stored - rows * LOCAL) * B * B * k,
        bytes_accessed=4 * (stored - rows * LOCAL) * B * B,
    )(row_ptr, col_index, held, partial_image, *arrived)
    returned = exchange(*returns)
    partial_adjoint, squares = call(
        local_backward_kernel,
        "local_backward",
        [((k, unknowns), F32), ((k, B), F32)],
        [SMEM, VMEM, VMEM],
        flops=2 * rows * LOCAL * B * B * k,
        bytes_accessed=2 * rows * LOCAL * B * B,
    )(row_ptr, held, image)
    adjoint, packed = call(
        gram_kernel,
        "gram",
        [((k, unknowns), F32), ((devices, 4, B), F32)],
        [SMEM] + [VMEM] * 8,
    )(send_list, partial_adjoint, squares, *returned)
    everywhere = lax.all_to_all(packed, AXES, 0, 0)
    basis, factor, gain = call(
        functools.partial(solve_kernel, unknowns * devices),
        "solve",
        [((k, unknowns), F32), ((k, k), F32), ((1, k), F32)],
        [VMEM, VMEM],
    )(everywhere, adjoint)
    return basis, factor, gain[0]


def solution(mesh):
    return jax.shard_map(
        local,
        mesh=mesh,
        in_specs=(
            P(AXES, None, None),
            P(None, AXES),
            P(AXES, None),
            P(AXES, None),
            P(AXES, None, None),
        ),
        out_specs=(P(None, AXES), P(), P()),
        check_vma=False,
    )
```

```python
import functools

import jax
import jax.numpy as jnp
from jax import lax
from jax.experimental import pallas as pl
from jax.experimental.pallas import tpu as pltpu
from jax.sharding import PartitionSpec as P

AXES = ("dom", "sub")
B = 128
SHORT = 5
LONG = 9
LOCAL = 3
F32 = jnp.float32
BF16 = jnp.bfloat16
BY_LAST = (((1,), (1,)), ((), ()))
BY_FIRST = (((1,), (0,)), ((), ()))
VMEM = pl.BlockSpec(memory_space=pltpu.VMEM)
SMEM = pl.BlockSpec(memory_space=pltpu.SMEM)
HBM = pl.BlockSpec(memory_space=pltpu.HBM)
LIMIT = 8 * 2**20


def neighbour(a, b):
    place = (a + 1) * 3 + b + 1
    return place - (place > 4)


def outward():
    return 2 * lax.rem(lax.axis_index("sub"), 2) - 1


def columns(block_row):
    return pl.ds(pl.multiple_of(block_row * B, B), B)


def joined(ref, places, axis):
    return jnp.concatenate([ref[place] for place in places], axis=axis)


def sent(s):
    return (
        ((0, -s), (1, -s), (-1, -s)),
        ((0, s),),
        ((s, s),),
        ((-s, s),),
        ((1, 0),),
        ((-1, 0),),
    )


def received(s):
    return (
        ((0, s),),
        ((0, -s),),
        ((-s, -s),),
        ((s, -s),),
        ((1, 0), (1, s)),
        ((-1, 0), (-1, s)),
    )


def exchange(pair, side, outer, inner, up, down):
    n_inner = lax.axis_size("sub")
    devices = lax.axis_size("dom") * n_inner

    def move(array, odd, even):
        return lax.ppermute(
            array,
            AXES,
            [(d, (d + (odd if d % 2 else even)) % devices) for d in range(devices)],
        )

    pair = move(pair, -1, 1)
    side = move(side, 1, -1)
    outer = move(outer, n_inner + 1, -n_inner - 1)
    inner = move(inner, 1 - n_inner, n_inner - 1)
    up = move(jnp.concatenate([up, pair[1:2]], axis=0), n_inner, n_inner)
    down = move(jnp.concatenate([down, pair[2:3]], axis=0), -n_inner, -n_inner)
    return pair, side, outer, inner, up, down


def gather_kernel(send_hbm, vectors_hbm, ptr_hbm, col_hbm, vectors, ptr, col, send_out, *refs):
    outgoing, (send, sems) = refs[:6], refs[6:]
    copies = [
        pltpu.make_async_copy(source, target, sems.at[i])
        for i, (source, target) in enumerate(
            (
                (send_hbm, send),
                (vectors_hbm, vectors),
                (ptr_hbm, ptr),
                (col_hbm, col),
                (send_hbm, send_out),
            )
        )
    ]
    for copy in copies:
        copy.start()
    for copy in copies:
        copy.wait()
    for ref, offsets in zip(outgoing, sent(outward())):
        for i, (a, b) in enumerate(offsets):
            for g in range(ref.shape[1]):
                ref[i, g] = vectors[:, columns(send[0, g, neighbour(a, b)])]


def local_forward_kernel(ptr, vectors, blocks_hbm, blocks, image, sems):
    rows = image.shape[0]
    parts = sems.shape[0]
    stored = blocks.shape[0]
    edges = [stored * i // parts for i in range(parts + 1)]
    copies = [
        pltpu.make_async_copy(blocks_hbm.at[a:b], blocks.at[a:b], sems.at[i])
        for i, (a, b) in enumerate(zip(edges[:-1], edges[1:]))
    ]
    for copy in copies:
        copy.start()
    waited = 0
    for j in range(rows):
        e = ptr[0, j]
        furthest = min(LONG * j, stored - SHORT * (rows - j)) + LOCAL
        while waited < parts and (j == rows - 1 or edges[waited] < furthest):
            copies[waited].wait()
            waited += 1
        near = [vectors[:, c * B : c * B + B] for c in (j, (j + 1) % rows, (j - 1) % rows)]
        image[j] = lax.dot_general(
            jnp.concatenate(near, axis=1),
            joined(blocks, [e + t for t in range(LOCAL)], 1),
            BY_LAST,
            preferred_element_type=F32,
        )


def ghost_kernel(ptr, col, blocks, partial_image, *refs):
    arrived, image, outgoing = refs[:6], refs[6], refs[7:13]
    ghosts, total, spread, long_rows = refs[13:]
    rows = image.shape[0]
    many = long_rows.shape[0] - 1
    s = outward()
    for ref, offsets in zip(arrived, received(s)):
        for i, (a, b) in enumerate(offsets):
            for g in range(ref.shape[1]):
                ghosts[neighbour(a, b) * ref.shape[1] + g] = ref[i, g]
    found = 0
    for j in range(rows):
        long_rows[jnp.minimum(found, many)] = j
        found = found + (ptr[0, j + 1] - ptr[0, j] > SHORT).astype(jnp.int32)

    def forward(e, first, last):
        return lax.dot_general(
            joined(ghosts, [col[0, e + t] - rows for t in range(first, last)], 1),
            joined(blocks, [e + t for t in range(first, last)], 1),
            BY_LAST,
            preferred_element_type=F32,
        )

    for j in range(rows):
        total[j] = partial_image[j] + forward(ptr[0, j], LOCAL, SHORT)
    for i in range(many):
        j = long_rows[i]
        total[j] += forward(ptr[0, j], SHORT, LONG)
    image[...] = total[...].astype(BF16)
    spread[...] = jnp.zeros_like(spread)
    banks = spread.shape[0]

    def backward(j, first, last):
        e = ptr[0, j]
        terms = lax.dot_general(
            image[j],
            joined(blocks, [e + t for t in range(first, last)], 1),
            BY_FIRST,
            preferred_element_type=F32,
        )
        for t in range(first, last):
            k = t - first
            spread[k % banks, col[0, e + t] - rows] += terms[:, k * B : k * B + B]

    for j in range(rows):
        backward(j, LOCAL, SHORT)
    for i in range(many):
        backward(long_rows[i], SHORT, LONG)
    for ref, offsets in zip(outgoing, sent(s)):
        for i, (a, b) in enumerate(offsets):
            for g in range(ref.shape[1]):
                slot = neighbour(-a, -b) * ref.shape[1] + g
                ref[i, g] = sum(spread[bank, slot] for bank in range(banks))


def local_backward_kernel(ptr, blocks, image, adjoint, squares):
    rows = image.shape[0]
    total = jnp.zeros(squares.shape, F32)
    for j in range(rows):
        before, after = (j - 1) % rows, (j + 1) % rows
        adjoint[:, j * B : j * B + B] = lax.dot_general(
            joined(image, [j, before, after], 1),
            joined(blocks, [ptr[0, j], ptr[0, before] + 1, ptr[0, after] + 2], 0),
            BY_FIRST,
            preferred_element_type=F32,
        )
        wide = image[j].astype(F32)
        total = total + wide * wide
    squares[...] = total


def group_masks(k):
    group = B // k
    row = lax.broadcasted_iota(jnp.int32, (k, B), 0)
    lane = lax.broadcasted_iota(jnp.int32, (k, B), 1)
    return lax.rem(row, group) == lax.div(lane, k), row, lane


def gram_kernel(send, partial_adjoint, squares, *refs):
    arrived, adjoint, packed = refs[:6], refs[6], refs[7]
    k = adjoint.shape[0]
    s = outward()
    adjoint[...] = partial_adjoint[...]
    for ref, offsets in zip(arrived, received(s)):
        for i, (a, b) in enumerate(offsets):
            for g in range(ref.shape[1]):
                place = columns(send[0, g, neighbour(-a, -b)])
                adjoint[:, place] += ref[i, g]
    z = adjoint[...]
    gram = lax.dot_general(z, z, BY_LAST, precision=lax.Precision.HIGHEST, preferred_element_type=F32)
    own, row, lane = group_masks(k)
    tile = (lax.rem(lane, k) == row).astype(F32)
    tiled = lax.dot_general(gram, tile, BY_FIRST, precision=lax.Precision.HIGHEST, preferred_element_type=F32)
    tiled = jnp.where(own, tiled, 0.0)
    group = B // k
    lines = [jnp.sum(tiled[i : i + group], axis=0, keepdims=True) for i in range(0, k, group)]
    norms = jnp.sum(squares[...], axis=1, keepdims=True)
    lines.append(jnp.sum(jnp.where(lane == row, norms, 0.0), axis=0, keepdims=True))
    lines.append(jnp.zeros(((-len(lines)) % 4, B), F32))
    packed[...] = jnp.broadcast_to(jnp.concatenate(lines, axis=0)[None], packed.shape)


def solve_kernel(count, packed, adjoint, basis, factor, gain):
    k = adjoint.shape[0]
    group = B // k
    own, row, lane = group_masks(k)
    sums = jnp.sum(packed[...], axis=0) / count
    spread = jnp.concatenate(
        [jnp.broadcast_to(sums[i : i + 1], (group, B)) for i in range(k // group)], axis=0
    )
    line = lax.broadcasted_iota(jnp.int32, (B, B), 0)
    column = lax.broadcasted_iota(jnp.int32, (B, B), 1)
    fold = (lax.rem(line, k) == column).astype(F32)
    both = lax.dot_general(
        jnp.where(own, spread, 0.0), fold, BY_FIRST, precision=lax.Precision.HIGHEST, preferred_element_type=F32
    )
    both = both + (lane == row + k).astype(F32)
    for i in range(k):
        pivots = jnp.broadcast_to(both[:, i : i + 1], (k, B))
        scale = lax.rsqrt(pivots[i : i + 1])
        top = both[i : i + 1] * scale
        lower = both - pivots * scale * top
        both = jnp.where(row > i, lower, jnp.where(row == i, top, both))
    factor[...] = jnp.where(lane >= row, both, 0.0)[:, :k]
    gain[...] = sums[k // group : k // group + 1, :k]
    inverse = both[:, k : 2 * k]
    basis[...] = lax.dot_general(
        inverse, adjoint[...], BY_FIRST, precision=lax.Precision.HIGHEST, preferred_element_type=F32
    )


def call(kernel, name, shapes, in_specs, scratch=(), flops=0, bytes_accessed=0):
    return pl.pallas_call(
        kernel,
        name=name,
        out_shape=[jax.ShapeDtypeStruct(*s) if isinstance(s, tuple) else s for s in shapes],
        in_specs=in_specs,
        out_specs=[VMEM] * len(shapes),
        scratch_shapes=scratch,
        compiler_params=pltpu.CompilerParams(vmem_limit_bytes=LIMIT),
        cost_estimate=pl.CostEstimate(flops=flops, bytes_accessed=bytes_accessed, transcendentals=0),
    )


def local(blocks, vectors, col_index, row_ptr, send_list):
    k, unknowns = vectors.shape
    rows = unknowns // B
    stored = blocks.shape[0]
    devices = lax.axis_size("dom") * lax.axis_size("sub")
    ghost = send_list.shape[2]
    slots = send_list.shape[1] * ghost
    many = (stored - SHORT * rows) // (LONG - SHORT)
    sizes = (3, 1, 1, 1, 1, 1)
    send_lines = jnp.transpose(send_list, (0, 2, 1))
    here, ptr, col, send, *outgoing = call(
        gather_kernel,
        "gather",
        [(vectors.shape, BF16)]
        + [(a.shape, jnp.int32) for a in (row_ptr, col_index, send_lines)]
        + [((n, ghost, k, B), BF16) for n in sizes],
        [HBM] * 4,
        scratch=[pltpu.SMEM(send_lines.shape, jnp.int32), pltpu.SemaphoreType.DMA((5,))],
        bytes_accessed=0,
    )(*[pltpu.with_memory_space_constraint(a, pltpu.HBM) for a in (send_lines, vectors, row_ptr, col_index)])
    arrived = exchange(*outgoing)
    held, partial_image = call(
        local_forward_kernel,
        "local_forward",
        [pltpu.VMEM(blocks.shape, BF16), ((rows, k, B), F32)],
        [SMEM, VMEM, HBM],
        scratch=[pltpu.SemaphoreType.DMA((8,))],
        flops=2 * rows * LOCAL * B * B * k,
        bytes_accessed=2 * rows * LOCAL * B * B,
    )(ptr, here, pltpu.with_memory_space_constraint(blocks, pltpu.HBM))
    image, *returns = call(
        ghost_kernel,
        "ghost",
        [((rows, k, B), BF16)] + [((n, ghost, k, B), F32) for n in sizes],
        [SMEM, SMEM] + [VMEM] * 8,
        scratch=[
            pltpu.VMEM((slots, k, B), BF16),
            pltpu.VMEM((rows, k, B), F32),
            pltpu.VMEM((4, slots, k, B), F32),
            pltpu.SMEM((many + 1,), jnp.int32),
        ],
        flops=4 * (stored - rows * LOCAL) * B * B * k,
        bytes_accessed=4 * (stored - rows * LOCAL) * B * B,
    )(ptr, col, held, partial_image, *arrived)
    returned = exchange(*returns)
    partial_adjoint, squares = call(
        local_backward_kernel,
        "local_backward",
        [((k, unknowns), F32), ((k, B), F32)],
        [SMEM, VMEM, VMEM],
        flops=2 * rows * LOCAL * B * B * k,
        bytes_accessed=2 * rows * LOCAL * B * B,
    )(ptr, held, image)
    adjoint, packed = call(
        gram_kernel,
        "gram",
        [((k, unknowns), F32), ((devices, 4, B), F32)],
        [SMEM] + [VMEM] * 8,
    )(send, partial_adjoint, squares, *returned)
    everywhere = lax.all_to_all(packed, AXES, 0, 0)
    basis, factor, gain = call(
        functools.partial(solve_kernel, unknowns * devices),
        "solve",
        [((k, unknowns), F32), ((k, k), F32), ((1, k), F32)],
        [VMEM, VMEM],
    )(everywhere, adjoint)
    return basis, factor, gain[0]


def solution(mesh):
    return jax.shard_map(
        local,
        mesh=mesh,
        in_specs=(
            P(AXES, None, None),
            P(None, AXES),
            P(AXES, None),
            P(AXES, None),
            P(AXES, None, None),
        ),
        out_specs=(P(None, AXES), P(), P()),
        check_vma=False,
    )
```

```python
import functools

import jax
import jax.numpy as jnp
from jax import lax
from jax.experimental import pallas as pl
from jax.experimental.pallas import tpu as pltpu
from jax.sharding import PartitionSpec as P

AXES = ("dom", "sub")
B = 128
SHORT = 5
LONG = 9
LOCAL = 3
F32 = jnp.float32
BF16 = jnp.bfloat16
BY_LAST = (((1,), (1,)), ((), ()))
BY_FIRST = (((1,), (0,)), ((), ()))
VMEM = pl.BlockSpec(memory_space=pltpu.VMEM)
SMEM = pl.BlockSpec(memory_space=pltpu.SMEM)
ANY = pl.BlockSpec(memory_space=pl.ANY)
HBM = pl.BlockSpec(memory_space=pltpu.HBM)
LIMIT = 8 * 2**20


def neighbour(a, b):
    place = (a + 1) * 3 + b + 1
    return place - (place > 4)


def outward():
    return 2 * lax.rem(lax.axis_index("sub"), 2) - 1


def columns(block_row):
    return pl.ds(pl.multiple_of(block_row * B, B), B)


def joined(ref, places, axis):
    return jnp.concatenate([ref[place] for place in places], axis=axis)


def sent(s):
    return (
        ((0, -s), (1, -s), (-1, -s)),
        ((0, s),),
        ((s, s),),
        ((-s, s),),
        ((1, 0),),
        ((-1, 0),),
    )


def received(s):
    return (
        ((0, s),),
        ((0, -s),),
        ((-s, -s),),
        ((s, -s),),
        ((1, 0), (1, s)),
        ((-1, 0), (-1, s)),
    )


def exchange(pair, side, outer, inner, up, down):
    n_inner = lax.axis_size("sub")
    devices = lax.axis_size("dom") * n_inner

    def move(array, odd, even):
        return lax.ppermute(
            array,
            AXES,
            [(d, (d + (odd if d % 2 else even)) % devices) for d in range(devices)],
        )

    pair = move(pair, -1, 1)
    side = move(side, 1, -1)
    outer = move(outer, n_inner + 1, -n_inner - 1)
    inner = move(inner, 1 - n_inner, n_inner - 1)
    up = move(jnp.concatenate([up, pair[1:2]], axis=0), n_inner, n_inner)
    down = move(jnp.concatenate([down, pair[2:3]], axis=0), -n_inner, -n_inner)
    return pair, side, outer, inner, up, down


def gather_kernel(send_hbm, vectors_hbm, ptr_hbm, col_hbm, blocks_hbm, vectors, ptr, col, send_out, *refs):
    outgoing, (send, sems) = refs[:6], refs[6:]
    copies = [
        pltpu.make_async_copy(source, target, sems.at[i])
        for i, (source, target) in enumerate(
            (
                (send_hbm, send),
                (vectors_hbm, vectors),
                (ptr_hbm, ptr),
                (col_hbm, col),
                (send_hbm, send_out),
            )
        )
    ]
    for copy in copies:
        copy.start()
    for copy in copies:
        copy.wait()
    for ref, offsets in zip(outgoing, sent(outward())):
        for i, (a, b) in enumerate(offsets):
            for g in range(ref.shape[1]):
                ref[i, g] = vectors[:, columns(send[0, g, neighbour(a, b)])]
        for i in range(len(offsets), ref.shape[0]):
            ref[i] = ref[0]


def local_forward_kernel(ptr, vectors, blocks, *refs):
    image = refs[-1]
    rows = image.shape[0]
    for j in range(rows):
        e = ptr[0, j]
        near = [vectors[:, c * B : c * B + B] for c in (j, (j + 1) % rows, (j - 1) % rows)]
        image[j] = lax.dot_general(
            jnp.concatenate(near, axis=1),
            joined(blocks, [e + t for t in range(LOCAL)], 1),
            BY_LAST,
            preferred_element_type=F32,
        )


def ghost_kernel(ptr, col, blocks, partial_image, *refs):
    arrived, image, outgoing = refs[:6], refs[6], refs[7:13]
    ghosts, total, spread, long_rows = refs[13:]
    rows = image.shape[0]
    many = long_rows.shape[0] - 1
    s = outward()
    for ref, offsets in zip(arrived, received(s)):
        for i, (a, b) in enumerate(offsets):
            for g in range(ref.shape[1]):
                ghosts[neighbour(a, b) * ref.shape[1] + g] = ref[i, g]
    found = 0
    for j in range(rows):
        long_rows[jnp.minimum(found, many)] = j
        found = found + (ptr[0, j + 1] - ptr[0, j] > SHORT).astype(jnp.int32)

    def forward(e, first, last):
        return lax.dot_general(
            joined(ghosts, [col[0, e + t] - rows for t in range(first, last)], 1),
            joined(blocks, [e + t for t in range(first, last)], 1),
            BY_LAST,
            preferred_element_type=F32,
        )

    for j in range(rows):
        total[j] = partial_image[j] + forward(ptr[0, j], LOCAL, SHORT)
    for i in range(many):
        j = long_rows[i]
        total[j] += forward(ptr[0, j], SHORT, LONG)
    image[...] = total[...].astype(BF16)
    spread[...] = jnp.zeros_like(spread)
    banks = spread.shape[0]

    def backward(j, first, last):
        e = ptr[0, j]
        terms = lax.dot_general(
            image[j],
            joined(blocks, [e + t for t in range(first, last)], 1),
            BY_FIRST,
            preferred_element_type=F32,
        )
        for t in range(first, last):
            k = t - first
            spread[k % banks, col[0, e + t] - rows] += terms[:, k * B : k * B + B]

    for j in range(rows):
        backward(j, LOCAL, SHORT)
    for i in range(many):
        backward(long_rows[i], SHORT, LONG)
    for ref, offsets in zip(outgoing, sent(s)):
        for i, (a, b) in enumerate(offsets):
            for g in range(ref.shape[1]):
                slot = neighbour(-a, -b) * ref.shape[1] + g
                ref[i, g] = sum(spread[bank, slot] for bank in range(banks))
        for i in range(len(offsets), ref.shape[0]):
            ref[i] = ref[0]


def local_backward_kernel(ptr, blocks, image, adjoint, squares):
    rows = image.shape[0]
    total = jnp.zeros(squares.shape, F32)
    for j in range(rows):
        before, after = (j - 1) % rows, (j + 1) % rows
        adjoint[:, j * B : j * B + B] = lax.dot_general(
            joined(image, [j, before, after], 1),
            joined(blocks, [ptr[0, j], ptr[0, before] + 1, ptr[0, after] + 2], 0),
            BY_FIRST,
            preferred_element_type=F32,
        )
        wide = image[j].astype(F32)
        total = total + wide * wide
    squares[...] = total


def group_masks(k):
    group = B // k
    row = lax.broadcasted_iota(jnp.int32, (k, B), 0)
    lane = lax.broadcasted_iota(jnp.int32, (k, B), 1)
    return lax.rem(row, group) == lax.div(lane, k), row, lane


def gram_kernel(send, partial_adjoint, squares, *refs):
    arrived, adjoint, packed = refs[:6], refs[6], refs[7]
    k = adjoint.shape[0]
    s = outward()
    adjoint[...] = partial_adjoint[...]
    for ref, offsets in zip(arrived, received(s)):
        for i, (a, b) in enumerate(offsets):
            for g in range(ref.shape[1]):
                place = columns(send[0, g, neighbour(-a, -b)])
                adjoint[:, place] += ref[i, g]
    z = adjoint[...]
    gram = lax.dot_general(z, z, BY_LAST, precision=lax.Precision.HIGHEST, preferred_element_type=F32)
    own, row, lane = group_masks(k)
    tile = (lax.rem(lane, k) == row).astype(F32)
    tiled = lax.dot_general(gram, tile, BY_FIRST, precision=lax.Precision.HIGHEST, preferred_element_type=F32)
    tiled = jnp.where(own, tiled, 0.0)
    group = B // k
    lines = [jnp.sum(tiled[i : i + group], axis=0, keepdims=True) for i in range(0, k, group)]
    norms = jnp.sum(squares[...], axis=1, keepdims=True)
    lines.append(jnp.sum(jnp.where(lane == row, norms, 0.0), axis=0, keepdims=True))
    lines.append(jnp.zeros(((-len(lines)) % 4, B), F32))
    packed[...] = jnp.broadcast_to(jnp.concatenate(lines, axis=0)[None], packed.shape)


def solve_kernel(count, packed, adjoint, basis, factor, gain):
    k = adjoint.shape[0]
    group = B // k
    own, row, lane = group_masks(k)
    sums = jnp.sum(packed[...], axis=0) / count
    spread = jnp.concatenate(
        [jnp.broadcast_to(sums[i : i + 1], (group, B)) for i in range(k // group)], axis=0
    )
    line = lax.broadcasted_iota(jnp.int32, (B, B), 0)
    column = lax.broadcasted_iota(jnp.int32, (B, B), 1)
    fold = (lax.rem(line, k) == column).astype(F32)
    both = lax.dot_general(
        jnp.where(own, spread, 0.0), fold, BY_FIRST, precision=lax.Precision.HIGHEST, preferred_element_type=F32
    )
    both = both + (lane == row + k).astype(F32)
    for i in range(k):
        pivots = jnp.broadcast_to(both[:, i : i + 1], (k, B))
        scale = lax.rsqrt(pivots[i : i + 1])
        top = both[i : i + 1] * scale
        lower = both - pivots * scale * top
        both = jnp.where(row > i, lower, jnp.where(row == i, top, both))
    factor[...] = jnp.where(lane >= row, both, 0.0)[:, :k]
    gain[...] = sums[k // group : k // group + 1, :k]
    inverse = both[:, k : 2 * k]
    basis[...] = lax.dot_general(
        inverse, adjoint[...], BY_FIRST, precision=lax.Precision.HIGHEST, preferred_element_type=F32
    )


def call(kernel, name, shapes, in_specs, scratch=(), flops=0, bytes_accessed=0):
    return pl.pallas_call(
        kernel,
        name=name,
        out_shape=[jax.ShapeDtypeStruct(*s) if isinstance(s, tuple) else s for s in shapes],
        in_specs=in_specs,
        out_specs=[VMEM] * len(shapes),
        scratch_shapes=scratch,
        compiler_params=pltpu.CompilerParams(vmem_limit_bytes=LIMIT),
        cost_estimate=pl.CostEstimate(flops=flops, bytes_accessed=bytes_accessed, transcendentals=0),
    )


def local(blocks, vectors, col_index, row_ptr, send_list):
    k, unknowns = vectors.shape
    rows = unknowns // B
    stored = blocks.shape[0]
    devices = lax.axis_size("dom") * lax.axis_size("sub")
    ghost = send_list.shape[2]
    slots = send_list.shape[1] * ghost
    many = (stored - SHORT * rows) // (LONG - SHORT)
    sizes = (3, 2, 2, 2, 1, 1)
    send_lines = jnp.transpose(send_list, (0, 2, 1))
    here, ptr, col, send, *outgoing = call(
        gather_kernel,
        "gather",
        [(vectors.shape, BF16)]
        + [(a.shape, jnp.int32) for a in (row_ptr, col_index, send_lines)]
        + [((n, ghost, k, B), BF16) for n in sizes],
        [HBM] * 5,
        scratch=[pltpu.SMEM(send_lines.shape, jnp.int32), pltpu.SemaphoreType.DMA((5,))],
        bytes_accessed=0,
    )(*[pltpu.with_memory_space_constraint(a, pltpu.HBM) for a in (send_lines, vectors, row_ptr, col_index, blocks)])
    arrived = exchange(*outgoing)
    (partial_image,) = call(
        local_forward_kernel,
        "local_forward",
        [((rows, k, B), F32)],
        [SMEM, VMEM, VMEM] + [ANY] * len(arrived[:0]),
        flops=2 * rows * LOCAL * B * B * k,
        bytes_accessed=2 * rows * LOCAL * B * B,
    )(ptr, here, blocks, *arrived[:0])
    image, *returns = call(
        ghost_kernel,
        "ghost",
        [((rows, k, B), BF16)] + [((n, ghost, k, B), F32) for n in sizes],
        [SMEM, SMEM] + [VMEM] * 8,
        scratch=[
            pltpu.VMEM((slots, k, B), BF16),
            pltpu.VMEM((rows, k, B), F32),
            pltpu.VMEM((4, slots, k, B), F32),
            pltpu.SMEM((many + 1,), jnp.int32),
        ],
        flops=4 * (stored - rows * LOCAL) * B * B * k,
        bytes_accessed=4 * (stored - rows * LOCAL) * B * B,
    )(ptr, col, blocks, partial_image, *arrived)
    returned = exchange(*returns)
    partial_adjoint, squares = call(
        local_backward_kernel,
        "local_backward",
        [((k, unknowns), F32), ((k, B), F32)],
        [SMEM, VMEM, VMEM],
        flops=2 * rows * LOCAL * B * B * k,
        bytes_accessed=2 * rows * LOCAL * B * B,
    )(ptr, blocks, image)
    adjoint, packed = call(
        gram_kernel,
        "gram",
        [((k, unknowns), F32), ((devices, 4, B), F32)],
        [SMEM] + [VMEM] * 8,
    )(send, partial_adjoint, squares, *returned)
    everywhere = lax.all_to_all(packed, AXES, 0, 0)
    basis, factor, gain = call(
        functools.partial(solve_kernel, unknowns * devices),
        "solve",
        [((k, unknowns), F32), ((k, k), F32), ((1, k), F32)],
        [VMEM, VMEM],
    )(everywhere, adjoint)
    return basis, factor, gain[0]


def solution(mesh):
    return jax.shard_map(
        local,
        mesh=mesh,
        in_specs=(
            P(AXES, None, None),
            P(None, AXES),
            P(AXES, None),
            P(AXES, None),
            P(AXES, None, None),
        ),
        out_specs=(P(None, AXES), P(), P()),
        check_vma=False,
    )
```

```python
import functools

import jax
import jax.numpy as jnp
from jax import lax
from jax.experimental import pallas as pl
from jax.experimental.pallas import tpu as pltpu
from jax.sharding import PartitionSpec as P

AXES = ("dom", "sub")
B = 128
SHORT = 5
LONG = 9
LOCAL = 3
F32 = jnp.float32
BF16 = jnp.bfloat16
BY_LAST = (((1,), (1,)), ((), ()))
BY_FIRST = (((1,), (0,)), ((), ()))
VMEM = pl.BlockSpec(memory_space=pltpu.VMEM)
SMEM = pl.BlockSpec(memory_space=pltpu.SMEM)
ANY = pl.BlockSpec(memory_space=pl.ANY)
HBM = pl.BlockSpec(memory_space=pltpu.HBM)
LIMIT = 8 * 2**20


def neighbour(a, b):
    place = (a + 1) * 3 + b + 1
    return place - (place > 4)


def directions():
    outer, inner = lax.axis_index("dom"), lax.axis_index("sub")
    past = (inner == lax.axis_size("sub") - 1).astype(jnp.int32)
    return 2 * lax.rem(inner, 2) - 1, 1 - 2 * lax.rem(outer + past, 2), 1 - 2 * lax.rem(outer, 2)


def columns(block_row):
    return pl.ds(pl.multiple_of(block_row * B, B), B)


def joined(ref, places, axis):
    return jnp.concatenate([ref[place] for place in places], axis=axis)


def sent(s, t, u):
    return (
        ((0, -s), (u, -s), (-u, -s)),
        ((-t, s),),
        ((0, s),),
        ((t, s),),
        ((-u, 0),),
        ((u, 0),),
    )


def received(s, t, u):
    return (
        ((0, s),),
        ((t, -s),),
        ((0, -s),),
        ((-t, -s),),
        ((u, 0), (u, s)),
        ((-u, 0), (-u, s)),
    )


def exchange(pair, cross_far, side, cross_near, far, near):
    n_inner = lax.axis_size("sub")
    devices = lax.axis_size("dom") * n_inner

    def swap(array, target):
        return lax.ppermute(array, AXES, [(d, target(d) % devices) for d in range(devices)])

    def step(d):
        return 1 if d % 2 else -1

    def towards(d):
        return n_inner if (d // n_inner) % 2 == 0 else -n_inner

    def diagonal(d, sign):
        past = (d + d % 2) % devices
        return d + step(d) + sign * towards(past)

    pair = swap(pair, lambda d: d - step(d))
    cross_far = swap(cross_far, lambda d: diagonal(d, -1))
    side = swap(side, lambda d: d + step(d))
    cross_near = swap(cross_near, lambda d: diagonal(d, 1))
    far = swap(jnp.concatenate([far, pair[2:3]], axis=0), lambda d: d - towards(d))
    near = swap(jnp.concatenate([near, pair[1:2]], axis=0), lambda d: d + towards(d))
    return pair, cross_far, side, cross_near, far, near


def gather_kernel(send_hbm, vectors_hbm, ptr_hbm, col_hbm, blocks_hbm, vectors, ptr, col, send_out, *refs):
    outgoing, (send, sems) = refs[:6], refs[6:]
    copies = [
        pltpu.make_async_copy(source, target, sems.at[i])
        for i, (source, target) in enumerate(
            (
                (send_hbm, send),
                (vectors_hbm, vectors),
                (ptr_hbm, ptr),
                (col_hbm, col),
                (send_hbm, send_out),
            )
        )
    ]
    for copy in copies:
        copy.start()
    for copy in copies:
        copy.wait()
    for ref, offsets in zip(outgoing, sent(*directions())):
        for i, (a, b) in enumerate(offsets):
            for g in range(ref.shape[1]):
                ref[i, g] = vectors[:, columns(send[0, g, neighbour(a, b)])]
        for i in range(len(offsets), ref.shape[0]):
            ref[i] = ref[0]


def local_forward_kernel(ptr, vectors, blocks, *refs):
    image = refs[-1]
    rows = image.shape[0]
    for j in range(rows):
        e = ptr[0, j]
        near = [vectors[:, c * B : c * B + B] for c in (j, (j + 1) % rows, (j - 1) % rows)]
        image[j] = lax.dot_general(
            jnp.concatenate(near, axis=1),
            joined(blocks, [e + t for t in range(LOCAL)], 1),
            BY_LAST,
            preferred_element_type=F32,
        )


def ghost_kernel(ptr, col, blocks, partial_image, *refs):
    arrived, image, outgoing = refs[:6], refs[6], refs[7:13]
    ghosts, total, spread, long_rows = refs[13:]
    rows = image.shape[0]
    many = long_rows.shape[0] - 1
    way = directions()
    for ref, offsets in zip(arrived, received(*way)):
        for i, (a, b) in enumerate(offsets):
            for g in range(ref.shape[1]):
                ghosts[neighbour(a, b) * ref.shape[1] + g] = ref[i, g]
    found = 0
    for j in range(rows):
        long_rows[jnp.minimum(found, many)] = j
        found = found + (ptr[0, j + 1] - ptr[0, j] > SHORT).astype(jnp.int32)

    def forward(e, first, last):
        return lax.dot_general(
            joined(ghosts, [col[0, e + t] - rows for t in range(first, last)], 1),
            joined(blocks, [e + t for t in range(first, last)], 1),
            BY_LAST,
            preferred_element_type=F32,
        )

    for j in range(rows):
        total[j] = partial_image[j] + forward(ptr[0, j], LOCAL, SHORT)
    for i in range(many):
        j = long_rows[i]
        total[j] += forward(ptr[0, j], SHORT, LONG)
    image[...] = total[...].astype(BF16)
    spread[...] = jnp.zeros_like(spread)
    banks = spread.shape[0]

    def backward(j, first, last):
        e = ptr[0, j]
        terms = lax.dot_general(
            image[j],
            joined(blocks, [e + t for t in range(first, last)], 1),
            BY_FIRST,
            preferred_element_type=F32,
        )
        for t in range(first, last):
            k = t - first
            spread[k % banks, col[0, e + t] - rows] += terms[:, k * B : k * B + B]

    for j in range(rows):
        backward(j, LOCAL, SHORT)
    for i in range(many):
        backward(long_rows[i], SHORT, LONG)
    for ref, offsets in zip(outgoing, sent(*way)):
        for i, (a, b) in enumerate(offsets):
            for g in range(ref.shape[1]):
                slot = neighbour(-a, -b) * ref.shape[1] + g
                ref[i, g] = sum(spread[bank, slot] for bank in range(banks))
        for i in range(len(offsets), ref.shape[0]):
            ref[i] = ref[0]


def local_backward_kernel(ptr, blocks, image, adjoint, squares):
    rows = image.shape[0]
    total = jnp.zeros(squares.shape, F32)
    for j in range(rows):
        before, after = (j - 1) % rows, (j + 1) % rows
        adjoint[:, j * B : j * B + B] = lax.dot_general(
            joined(image, [j, before, after], 1),
            joined(blocks, [ptr[0, j], ptr[0, before] + 1, ptr[0, after] + 2], 0),
            BY_FIRST,
            preferred_element_type=F32,
        )
        wide = image[j].astype(F32)
        total = total + wide * wide
    squares[...] = total


def group_masks(k):
    group = B // k
    row = lax.broadcasted_iota(jnp.int32, (k, B), 0)
    lane = lax.broadcasted_iota(jnp.int32, (k, B), 1)
    return lax.rem(row, group) == lax.div(lane, k), row, lane


def gram_kernel(send, partial_adjoint, squares, *refs):
    arrived, adjoint, packed = refs[:6], refs[6], refs[7]
    k = adjoint.shape[0]
    way = directions()
    adjoint[...] = partial_adjoint[...]
    for ref, offsets in zip(arrived, received(*way)):
        for i, (a, b) in enumerate(offsets):
            for g in range(ref.shape[1]):
                place = columns(send[0, g, neighbour(-a, -b)])
                adjoint[:, place] += ref[i, g]
    z = adjoint[...]
    gram = lax.dot_general(z, z, BY_LAST, precision=lax.Precision.HIGHEST, preferred_element_type=F32)
    own, row, lane = group_masks(k)
    tile = (lax.rem(lane, k) == row).astype(F32)
    tiled = lax.dot_general(gram, tile, BY_FIRST, precision=lax.Precision.HIGHEST, preferred_element_type=F32)
    tiled = jnp.where(own, tiled, 0.0)
    group = B // k
    lines = [jnp.sum(tiled[i : i + group], axis=0, keepdims=True) for i in range(0, k, group)]
    norms = jnp.sum(squares[...], axis=1, keepdims=True)
    lines.append(jnp.sum(jnp.where(lane == row, norms, 0.0), axis=0, keepdims=True))
    lines.append(jnp.zeros(((-len(lines)) % 4, B), F32))
    packed[...] = jnp.broadcast_to(jnp.concatenate(lines, axis=0)[None], packed.shape)


def solve_kernel(count, packed, adjoint, basis, factor, gain):
    k = adjoint.shape[0]
    group = B // k
    own, row, lane = group_masks(k)
    sums = jnp.sum(packed[...], axis=0) / count
    spread = jnp.concatenate(
        [jnp.broadcast_to(sums[i : i + 1], (group, B)) for i in range(k // group)], axis=0
    )
    line = lax.broadcasted_iota(jnp.int32, (B, B), 0)
    column = lax.broadcasted_iota(jnp.int32, (B, B), 1)
    fold = (lax.rem(line, k) == column).astype(F32)
    both = lax.dot_general(
        jnp.where(own, spread, 0.0), fold, BY_FIRST, precision=lax.Precision.HIGHEST, preferred_element_type=F32
    )
    both = both + (lane == row + k).astype(F32)
    for i in range(k):
        pivots = jnp.broadcast_to(both[:, i : i + 1], (k, B))
        scale = lax.rsqrt(pivots[i : i + 1])
        top = both[i : i + 1] * scale
        lower = both - pivots * scale * top
        both = jnp.where(row > i, lower, jnp.where(row == i, top, both))
    factor[...] = jnp.where(lane >= row, both, 0.0)[:, :k]
    gain[...] = sums[k // group : k // group + 1, :k]
    inverse = both[:, k : 2 * k]
    basis[...] = lax.dot_general(
        inverse, adjoint[...], BY_FIRST, precision=lax.Precision.HIGHEST, preferred_element_type=F32
    )


def call(kernel, name, shapes, in_specs, scratch=(), flops=0, bytes_accessed=0):
    return pl.pallas_call(
        kernel,
        name=name,
        out_shape=[jax.ShapeDtypeStruct(*s) if isinstance(s, tuple) else s for s in shapes],
        in_specs=in_specs,
        out_specs=[VMEM] * len(shapes),
        scratch_shapes=scratch,
        compiler_params=pltpu.CompilerParams(vmem_limit_bytes=LIMIT),
        cost_estimate=pl.CostEstimate(flops=flops, bytes_accessed=bytes_accessed, transcendentals=0),
    )


def local(blocks, vectors, col_index, row_ptr, send_list):
    k, unknowns = vectors.shape
    rows = unknowns // B
    stored = blocks.shape[0]
    devices = lax.axis_size("dom") * lax.axis_size("sub")
    ghost = send_list.shape[2]
    slots = send_list.shape[1] * ghost
    many = (stored - SHORT * rows) // (LONG - SHORT)
    sizes = (3, 2, 2, 2, 1, 1)
    send_lines = jnp.transpose(send_list, (0, 2, 1))
    here, ptr, col, send, *outgoing = call(
        gather_kernel,
        "gather",
        [(vectors.shape, BF16)]
        + [(a.shape, jnp.int32) for a in (row_ptr, col_index, send_lines)]
        + [((n, ghost, k, B), BF16) for n in sizes],
        [HBM] * 5,
        scratch=[pltpu.SMEM(send_lines.shape, jnp.int32), pltpu.SemaphoreType.DMA((5,))],
        bytes_accessed=0,
    )(*[pltpu.with_memory_space_constraint(a, pltpu.HBM) for a in (send_lines, vectors, row_ptr, col_index, blocks)])
    arrived = exchange(*outgoing)
    (partial_image,) = call(
        local_forward_kernel,
        "local_forward",
        [((rows, k, B), F32)],
        [SMEM, VMEM, VMEM] + [ANY] * len(arrived[:0]),
        flops=2 * rows * LOCAL * B * B * k,
        bytes_accessed=2 * rows * LOCAL * B * B,
    )(ptr, here, blocks, *arrived[:0])
    image, *returns = call(
        ghost_kernel,
        "ghost",
        [((rows, k, B), BF16)] + [((n, ghost, k, B), F32) for n in sizes],
        [SMEM, SMEM] + [VMEM] * 8,
        scratch=[
            pltpu.VMEM((slots, k, B), BF16),
            pltpu.VMEM((rows, k, B), F32),
            pltpu.VMEM((4, slots, k, B), F32),
            pltpu.SMEM((many + 1,), jnp.int32),
        ],
        flops=4 * (stored - rows * LOCAL) * B * B * k,
        bytes_accessed=4 * (stored - rows * LOCAL) * B * B,
    )(ptr, col, blocks, partial_image, *arrived)
    returned = exchange(*returns)
    partial_adjoint, squares = call(
        local_backward_kernel,
        "local_backward",
        [((k, unknowns), F32), ((k, B), F32)],
        [SMEM, VMEM, VMEM],
        flops=2 * rows * LOCAL * B * B * k,
        bytes_accessed=2 * rows * LOCAL * B * B,
    )(ptr, blocks, image)
    adjoint, packed = call(
        gram_kernel,
        "gram",
        [((k, unknowns), F32), ((devices, 4, B), F32)],
        [SMEM] + [VMEM] * 8,
    )(send, partial_adjoint, squares, *returned)
    everywhere = lax.all_to_all(packed, AXES, 0, 0)
    basis, factor, gain = call(
        functools.partial(solve_kernel, unknowns * devices),
        "solve",
        [((k, unknowns), F32), ((k, k), F32), ((1, k), F32)],
        [VMEM, VMEM],
    )(everywhere, adjoint)
    return basis, factor, gain[0]


def solution(mesh):
    return jax.shard_map(
        local,
        mesh=mesh,
        in_specs=(
            P(AXES, None, None),
            P(None, AXES),
            P(AXES, None),
            P(AXES, None),
            P(AXES, None, None),
        ),
        out_specs=(P(None, AXES), P(), P()),
        check_vma=False,
    )
```

```python
import functools

import jax
import jax.numpy as jnp
from jax import lax
from jax.experimental import pallas as pl
from jax.experimental.pallas import tpu as pltpu
from jax.sharding import PartitionSpec as P

AXES = ("dom", "sub")
B = 128
SHORT = 5
LONG = 9
LOCAL = 3
F32 = jnp.float32
BF16 = jnp.bfloat16
BY_LAST = (((1,), (1,)), ((), ()))
BY_FIRST = (((1,), (0,)), ((), ()))
VMEM = pl.BlockSpec(memory_space=pltpu.VMEM)
SMEM = pl.BlockSpec(memory_space=pltpu.SMEM)
ANY = pl.BlockSpec(memory_space=pl.ANY)
HBM = pl.BlockSpec(memory_space=pltpu.HBM)
LIMIT = 8 * 2**20


def neighbour(a, b):
    place = (a + 1) * 3 + b + 1
    return place - (place > 4)


def directions():
    outer, inner = lax.axis_index("dom"), lax.axis_index("sub")
    past = (inner == lax.axis_size("sub") - 1).astype(jnp.int32)
    return 2 * lax.rem(inner, 2) - 1, 1 - 2 * lax.rem(outer + past, 2), 1 - 2 * lax.rem(outer, 2)


def columns(block_row):
    return pl.ds(pl.multiple_of(block_row * B, B), B)


def joined(ref, places, axis):
    return jnp.concatenate([ref[place] for place in places], axis=axis)


def sent(s, t, u):
    return (
        ((0, -s), (u, -s), (-u, -s)),
        ((-t, s),),
        ((0, s),),
        ((t, s),),
        ((-u, 0),),
        ((u, 0),),
    )


def received(s, t, u):
    return (
        ((0, s),),
        ((t, -s),),
        ((0, -s),),
        ((-t, -s),),
        ((u, 0), (u, s)),
        ((-u, 0), (-u, s)),
    )


def exchange(pair, cross_far, side, cross_near, far, near):
    n_inner = lax.axis_size("sub")
    devices = lax.axis_size("dom") * n_inner

    def swap(array, target):
        return lax.ppermute(array, AXES, [(d, target(d) % devices) for d in range(devices)])

    def step(d):
        return 1 if d % 2 else -1

    def towards(d):
        return n_inner if (d // n_inner) % 2 == 0 else -n_inner

    def diagonal(d, sign):
        past = (d + d % 2) % devices
        return d + step(d) + sign * towards(past)

    pair = swap(pair, lambda d: d - step(d))
    cross_far = swap(cross_far, lambda d: diagonal(d, -1))
    side = swap(side, lambda d: d + step(d))
    cross_near = swap(cross_near, lambda d: diagonal(d, 1))
    far = swap(jnp.concatenate([far, pair[2:3]], axis=0), lambda d: d - towards(d))
    near = swap(jnp.concatenate([near, pair[1:2]], axis=0), lambda d: d + towards(d))
    return pair, cross_far, side, cross_near, far, near


def rounded(size):
    return -(-size // B) * B


def gather_kernel(send_hbm, vectors_hbm, ptr_hbm, col_hbm, blocks_hbm, vectors, plan, send_lines, *refs):
    outgoing, (send, ptr, col, sems) = refs[:6], refs[6:]
    copies = [
        pltpu.make_async_copy(source, target, sems.at[i])
        for i, (source, target) in enumerate(
            (
                (send_hbm, send),
                (vectors_hbm, vectors),
                (ptr_hbm, ptr),
                (col_hbm, col),
                (send_hbm, send_lines),
            )
        )
    ]
    for copy in copies:
        copy.start()
    for copy in copies:
        copy.wait()
    for ref, offsets in zip(outgoing, sent(*directions())):
        for i, (a, b) in enumerate(offsets):
            for g in range(ref.shape[1]):
                ref[i, g] = vectors[:, columns(send[0, g, neighbour(a, b)])]
        for i in range(len(offsets), ref.shape[0]):
            ref[i] = ref[0]
    plan[:, : ptr.shape[1]] = ptr[...]
    plan[:, rounded(ptr.shape[1]) : rounded(ptr.shape[1]) + col.shape[1]] = col[...]


def local_forward_kernel(plan, vectors, blocks, *refs):
    image = refs[-1]
    rows = image.shape[0]
    for j in range(rows):
        e = plan[0, j]
        near = [vectors[:, c * B : c * B + B] for c in (j, (j + 1) % rows, (j - 1) % rows)]
        image[j] = lax.dot_general(
            jnp.concatenate(near, axis=1),
            joined(blocks, [e + t for t in range(LOCAL)], 1),
            BY_LAST,
            preferred_element_type=F32,
        )


def ghost_kernel(plan, blocks, partial_image, *refs):
    arrived, image, outgoing = refs[:6], refs[6], refs[7:13]
    ghosts, total, spread, long_rows = refs[13:]
    rows = image.shape[0]
    many = long_rows.shape[0] - 1
    first_column = rounded(rows + 1)
    way = directions()
    for ref, offsets in zip(arrived, received(*way)):
        for i, (a, b) in enumerate(offsets):
            for g in range(ref.shape[1]):
                ghosts[neighbour(a, b) * ref.shape[1] + g] = ref[i, g]
    found = 0
    for j in range(rows):
        long_rows[jnp.minimum(found, many)] = j
        found = found + (plan[0, j + 1] - plan[0, j] > SHORT).astype(jnp.int32)

    def forward(e, first, last):
        return lax.dot_general(
            joined(ghosts, [plan[0, first_column + e + t] - rows for t in range(first, last)], 1),
            joined(blocks, [e + t for t in range(first, last)], 1),
            BY_LAST,
            preferred_element_type=F32,
        )

    for j in range(rows):
        total[j] = partial_image[j] + forward(plan[0, j], LOCAL, SHORT)
    for i in range(many):
        j = long_rows[i]
        total[j] += forward(plan[0, j], SHORT, LONG)
    image[...] = total[...].astype(BF16)
    spread[...] = jnp.zeros_like(spread)
    banks = spread.shape[0]

    def backward(j, first, last):
        e = plan[0, j]
        terms = lax.dot_general(
            image[j],
            joined(blocks, [e + t for t in range(first, last)], 1),
            BY_FIRST,
            preferred_element_type=F32,
        )
        for t in range(first, last):
            k = t - first
            spread[k % banks, plan[0, first_column + e + t] - rows] += terms[:, k * B : k * B + B]

    for j in range(rows):
        backward(j, LOCAL, SHORT)
    for i in range(many):
        backward(long_rows[i], SHORT, LONG)
    for ref, offsets in zip(outgoing, sent(*way)):
        for i, (a, b) in enumerate(offsets):
            for g in range(ref.shape[1]):
                slot = neighbour(-a, -b) * ref.shape[1] + g
                ref[i, g] = sum(spread[bank, slot] for bank in range(banks))
        for i in range(len(offsets), ref.shape[0]):
            ref[i] = ref[0]


def local_backward_kernel(plan, blocks, image, adjoint, norms):
    rows, k = image.shape[:2]
    total = jnp.zeros((k, B), F32)
    for j in range(rows):
        before, after = (j - 1) % rows, (j + 1) % rows
        adjoint[:, j * B : j * B + B] = lax.dot_general(
            joined(image, [j, before, after], 1),
            joined(blocks, [plan[0, j], plan[0, before] + 1, plan[0, after] + 2], 0),
            BY_FIRST,
            preferred_element_type=F32,
        )
        wide = image[j].astype(F32)
        total = total + wide * wide
    row = lax.broadcasted_iota(jnp.int32, (k, B), 0)
    lane = lax.broadcasted_iota(jnp.int32, (k, B), 1)
    squares = jnp.sum(total, axis=1, keepdims=True)
    norms[...] = jnp.sum(jnp.where(lane == row, squares, 0.0), axis=0, keepdims=True)


def group_masks(k):
    group = B // k
    row = lax.broadcasted_iota(jnp.int32, (k, B), 0)
    lane = lax.broadcasted_iota(jnp.int32, (k, B), 1)
    return lax.rem(row, group) == lax.div(lane, k), row, lane


def gram_kernel(send, partial_adjoint, norms, *refs):
    arrived, adjoint, packed = refs[:6], refs[6], refs[7]
    k = adjoint.shape[0]
    way = directions()
    for ref, offsets in zip(arrived, received(*way)):
        for i, (a, b) in enumerate(offsets):
            for g in range(ref.shape[1]):
                place = columns(send[0, g, neighbour(-a, -b)])
                adjoint[:, place] += ref[i, g]
    z = adjoint[...]
    gram = lax.dot_general(z, z, BY_LAST, precision=lax.Precision.HIGHEST, preferred_element_type=F32)
    wide = jnp.concatenate([gram, jnp.zeros((k, B - k), F32)], axis=1)
    moved = pltpu.roll(wide, 0, 1, stride=k, stride_axis=0)
    group = B // k
    lines = [jnp.sum(moved[i : i + group], axis=0, keepdims=True) for i in range(0, k, group)]
    lines.append(norms[...])
    lines.append(jnp.zeros(((-len(lines)) % 4, B), F32))
    packed[...] = jnp.broadcast_to(jnp.concatenate(lines, axis=0)[None], packed.shape)


def solve_kernel(count, packed, adjoint, basis_hbm, factor_hbm, gain_hbm, basis, factor, gain, sems):
    k, unknowns = adjoint.shape
    group = B // k
    own, row, lane = group_masks(k)
    sums = jnp.sum(packed[...], axis=0) / count
    gain[...] = sums[k // group : k // group + 1, :k]
    small = [pltpu.make_async_copy(gain, gain_hbm, sems.at[0])]
    small[0].start()
    spread = jnp.concatenate(
        [jnp.broadcast_to(sums[i : i + 1], (group, B)) for i in range(k // group)], axis=0
    )
    gram = jnp.where(own, spread, 0.0)
    shift = k
    while shift < B:
        gram = gram + pltpu.roll(gram, shift, 1)
        shift *= 2
    lines = [jnp.broadcast_to(gram[:, i : i + 1], (k, B)) for i in range(k)]
    both = jnp.where(lane < k, gram, (lane == row + k).astype(F32))
    for i in range(k):
        scale = lax.rsqrt(lines[i][i : i + 1])
        left = lines[i] * scale
        top = both[i : i + 1] * scale
        for j in range(i + 1, k):
            lines[j] = lines[j] - left * left[j : j + 1]
        both = jnp.where(row > i, both - left * top, jnp.where(row == i, top, both))
    factor[...] = jnp.where(lane >= row, both, 0.0)[:, :k]
    small.append(pltpu.make_async_copy(factor, factor_hbm, sems.at[1]))
    small[1].start()
    inverse = both[:, k : 2 * k]
    parts = sems.shape[0] - 2
    copies = []
    for i in range(parts):
        place = pl.ds(i * (unknowns // parts), unknowns // parts)
        basis[:, place] = lax.dot_general(
            inverse,
            adjoint[:, place],
            BY_FIRST,
            precision=lax.Precision.HIGHEST,
            preferred_element_type=F32,
        )
        copies.append(pltpu.make_async_copy(basis.at[:, place], basis_hbm.at[:, place], sems.at[2 + i]))
        copies[-1].start()
    for copy in small + copies:
        copy.wait()


def call(kernel, name, shapes, in_specs, scratch=(), out=VMEM, alias={}, flops=0, bytes_accessed=0):
    return pl.pallas_call(
        kernel,
        name=name,
        out_shape=[jax.ShapeDtypeStruct(shape, dtype) for shape, dtype in shapes],
        in_specs=in_specs,
        out_specs=[out] * len(shapes),
        scratch_shapes=scratch,
        input_output_aliases=alias,
        compiler_params=pltpu.CompilerParams(vmem_limit_bytes=LIMIT),
        cost_estimate=pl.CostEstimate(flops=flops, bytes_accessed=bytes_accessed, transcendentals=0),
    )


def local(blocks, vectors, col_index, row_ptr, send_list):
    k, unknowns = vectors.shape
    rows = unknowns // B
    stored = blocks.shape[0]
    devices = lax.axis_size("dom") * lax.axis_size("sub")
    ghost = send_list.shape[2]
    slots = send_list.shape[1] * ghost
    many = (stored - SHORT * rows) // (LONG - SHORT)
    sizes = (3, 2, 2, 2, 1, 1)
    send_lines = jnp.transpose(send_list, (0, 2, 1))
    inputs = (send_lines, vectors, row_ptr, col_index, blocks)
    here, plan, send, *outgoing = call(
        gather_kernel,
        "gather",
        [(vectors.shape, BF16), ((1, rounded(rows + 1) + rounded(stored)), jnp.int32), (send_lines.shape, jnp.int32)]
        + [((n, ghost, k, B), BF16) for n in sizes],
        [HBM] * 5,
        scratch=[
            pltpu.SMEM(send_lines.shape, jnp.int32),
            pltpu.VMEM(row_ptr.shape, jnp.int32),
            pltpu.VMEM(col_index.shape, jnp.int32),
            pltpu.SemaphoreType.DMA((5,)),
        ],
    )(*[pltpu.with_memory_space_constraint(a, pltpu.HBM) for a in inputs])
    arrived = exchange(*outgoing)
    (partial_image,) = call(
        local_forward_kernel,
        "local_forward",
        [((rows, k, B), F32)],
        [SMEM, VMEM, VMEM],
        flops=2 * rows * LOCAL * B * B * k,
        bytes_accessed=2 * rows * LOCAL * B * B,
    )(plan, here, blocks)
    image, *returns = call(
        ghost_kernel,
        "ghost",
        [((rows, k, B), BF16)] + [((n, ghost, k, B), F32) for n in sizes],
        [SMEM] + [VMEM] * 8,
        scratch=[
            pltpu.VMEM((slots, k, B), BF16),
            pltpu.VMEM((rows, k, B), F32),
            pltpu.VMEM((4, slots, k, B), F32),
            pltpu.SMEM((many + 1,), jnp.int32),
        ],
        flops=4 * (stored - rows * LOCAL) * B * B * k,
        bytes_accessed=4 * (stored - rows * LOCAL) * B * B,
    )(plan, blocks, partial_image, *arrived)
    returned = exchange(*returns)
    partial_adjoint, norms = call(
        local_backward_kernel,
        "local_backward",
        [((k, unknowns), F32), ((1, B), F32)],
        [SMEM, VMEM, VMEM],
        flops=2 * rows * LOCAL * B * B * k,
        bytes_accessed=2 * rows * LOCAL * B * B,
    )(plan, blocks, image)
    adjoint, packed = call(
        gram_kernel,
        "gram",
        [((k, unknowns), F32), ((devices, 4, B), F32)],
        [SMEM] + [VMEM] * 8,
        alias={1: 0},
    )(send, partial_adjoint, norms, *returned)
    everywhere = lax.all_to_all(packed, AXES, 0, 0)
    parts = 4
    basis, factor, gain = call(
        functools.partial(solve_kernel, unknowns * devices),
        "solve",
        [((k, unknowns), F32), ((k, k), F32), ((1, k), F32)],
        [VMEM, VMEM],
        scratch=[
            pltpu.VMEM((k, unknowns), F32),
            pltpu.VMEM((k, k), F32),
            pltpu.VMEM((1, k), F32),
            pltpu.SemaphoreType.DMA((parts + 2,)),
        ],
        out=HBM,
    )(everywhere, adjoint)
    return basis, factor, gain[0]


def solution(mesh):
    return jax.shard_map(
        local,
        mesh=mesh,
        in_specs=(
            P(AXES, None, None),
            P(None, AXES),
            P(AXES, None),
            P(AXES, None),
            P(AXES, None, None),
        ),
        out_specs=(P(None, AXES), P(), P()),
        check_vma=False,
    )
```

```python
import functools

import jax
import jax.numpy as jnp
from jax import lax
from jax.experimental import pallas as pl
from jax.experimental.pallas import tpu as pltpu
from jax.sharding import PartitionSpec as P

AXES = ("dom", "sub")
B = 128
SHORT = 5
LONG = 9
LOCAL = 3
F32 = jnp.float32
BF16 = jnp.bfloat16
BY_LAST = (((1,), (1,)), ((), ()))
BY_FIRST = (((1,), (0,)), ((), ()))
VMEM = pl.BlockSpec(memory_space=pltpu.VMEM)
SMEM = pl.BlockSpec(memory_space=pltpu.SMEM)
ANY = pl.BlockSpec(memory_space=pl.ANY)
HBM = pl.BlockSpec(memory_space=pltpu.HBM)
LIMIT = 8 * 2**20


def neighbour(a, b):
    place = (a + 1) * 3 + b + 1
    return place - (place > 4)


def directions():
    outer, inner = lax.axis_index("dom"), lax.axis_index("sub")
    past = (inner == lax.axis_size("sub") - 1).astype(jnp.int32)
    return 2 * lax.rem(inner, 2) - 1, 1 - 2 * lax.rem(outer + past, 2), 1 - 2 * lax.rem(outer, 2)


def columns(block_row):
    return pl.ds(pl.multiple_of(block_row * B, B), B)


def joined(ref, places, axis):
    return jnp.concatenate([ref[place] for place in places], axis=axis)


def sent(s, t, u):
    return (
        ((0, -s), (u, -s), (-u, -s)),
        ((0, s),),
        ((-t, s),),
        ((t, s),),
        ((-u, 0),),
        ((u, 0),),
    )


def received(s, t, u):
    return (
        ((0, s),),
        ((0, -s),),
        ((t, -s),),
        ((-t, -s),),
        ((u, 0), (u, s)),
        ((-u, 0), (-u, s)),
    )


def exchange(pair, side, cross_far, cross_near, far, near):
    n_inner = lax.axis_size("sub")
    devices = lax.axis_size("dom") * n_inner

    def swap(array, target):
        return lax.ppermute(array, AXES, [(d, target(d) % devices) for d in range(devices)])

    def step(d):
        return 1 if d % 2 else -1

    def towards(d):
        return n_inner if (d // n_inner) % 2 == 0 else -n_inner

    def diagonal(d, sign):
        past = (d + d % 2) % devices
        return d + step(d) + sign * towards(past)

    pair = swap(pair, lambda d: d - step(d))
    side = swap(side, lambda d: d + step(d))
    cross_far = swap(cross_far, lambda d: diagonal(d, -1))
    cross_near = swap(cross_near, lambda d: diagonal(d, 1))
    far = swap(jnp.concatenate([far, pair[2:3]], axis=0), lambda d: d - towards(d))
    near = swap(jnp.concatenate([near, pair[1:2]], axis=0), lambda d: d + towards(d))
    return pair, side, cross_far, cross_near, far, near


def rounded(size):
    return -(-size // B) * B


def gather_kernel(send_hbm, vectors_hbm, ptr_hbm, col_hbm, blocks_hbm, vectors, plan, send_lines, *refs):
    outgoing, (send, ptr, col, sems) = refs[:6], refs[6:]
    copies = [
        pltpu.make_async_copy(source, target, sems.at[i])
        for i, (source, target) in enumerate(
            (
                (send_hbm, send),
                (vectors_hbm, vectors),
                (ptr_hbm, ptr),
                (col_hbm, col),
                (send_hbm, send_lines),
            )
        )
    ]
    for copy in copies:
        copy.start()
    for copy in copies:
        copy.wait()
    for ref, offsets in zip(outgoing, sent(*directions())):
        for i, (a, b) in enumerate(offsets):
            for g in range(ref.shape[1]):
                ref[i, g] = vectors[:, columns(send[0, g, neighbour(a, b)])]
        for i in range(len(offsets), ref.shape[0]):
            ref[i] = ref[0]
    plan[:, : ptr.shape[1]] = ptr[...]
    plan[:, rounded(ptr.shape[1]) : rounded(ptr.shape[1]) + col.shape[1]] = col[...]


def local_forward_kernel(plan, vectors, blocks, *refs):
    image = refs[-1]
    rows = image.shape[0]
    for j in range(rows):
        e = plan[0, j]
        near = [vectors[:, c * B : c * B + B] for c in (j, (j + 1) % rows, (j - 1) % rows)]
        image[j] = lax.dot_general(
            jnp.concatenate(near, axis=1),
            joined(blocks, [e + t for t in range(LOCAL)], 1),
            BY_LAST,
            preferred_element_type=F32,
        )


def ghost_kernel(plan, blocks, partial_image, *refs):
    arrived, image, outgoing = refs[:6], refs[6], refs[7:13]
    ghosts, total, spread, long_rows = refs[13:]
    rows = image.shape[0]
    many = long_rows.shape[0] - 1
    first_column = rounded(rows + 1)
    way = directions()
    for ref, offsets in zip(arrived, received(*way)):
        for i, (a, b) in enumerate(offsets):
            for g in range(ref.shape[1]):
                ghosts[neighbour(a, b) * ref.shape[1] + g] = ref[i, g]
    found = 0
    for j in range(rows):
        long_rows[jnp.minimum(found, many)] = j
        found = found + (plan[0, j + 1] - plan[0, j] > SHORT).astype(jnp.int32)

    def forward(e, first, last):
        return lax.dot_general(
            joined(ghosts, [plan[0, first_column + e + t] - rows for t in range(first, last)], 1),
            joined(blocks, [e + t for t in range(first, last)], 1),
            BY_LAST,
            preferred_element_type=F32,
        )

    for j in range(rows):
        total[j] = partial_image[j] + forward(plan[0, j], LOCAL, SHORT)
    for i in range(many):
        j = long_rows[i]
        total[j] += forward(plan[0, j], SHORT, LONG)
    image[...] = total[...].astype(BF16)
    spread[...] = jnp.zeros_like(spread)
    banks = spread.shape[0]

    def backward(j, first, last):
        e = plan[0, j]
        terms = lax.dot_general(
            image[j],
            joined(blocks, [e + t for t in range(first, last)], 1),
            BY_FIRST,
            preferred_element_type=F32,
        )
        for t in range(first, last):
            k = t - first
            spread[k % banks, plan[0, first_column + e + t] - rows] += terms[:, k * B : k * B + B]

    for j in range(rows):
        backward(j, LOCAL, SHORT)
    for i in range(many):
        backward(long_rows[i], SHORT, LONG)
    for ref, offsets in zip(outgoing, sent(*way)):
        for i, (a, b) in enumerate(offsets):
            for g in range(ref.shape[1]):
                slot = neighbour(-a, -b) * ref.shape[1] + g
                ref[i, g] = sum(spread[bank, slot] for bank in range(banks))
        for i in range(len(offsets), ref.shape[0]):
            ref[i] = ref[0]


def local_backward_kernel(plan, blocks, image, adjoint, norms):
    rows, k = image.shape[:2]
    total = jnp.zeros((k, B), F32)
    for j in range(rows):
        before, after = (j - 1) % rows, (j + 1) % rows
        adjoint[:, j * B : j * B + B] = lax.dot_general(
            joined(image, [j, before, after], 1),
            joined(blocks, [plan[0, j], plan[0, before] + 1, plan[0, after] + 2], 0),
            BY_FIRST,
            preferred_element_type=F32,
        )
        wide = image[j].astype(F32)
        total = total + wide * wide
    row = lax.broadcasted_iota(jnp.int32, (k, B), 0)
    lane = lax.broadcasted_iota(jnp.int32, (k, B), 1)
    squares = jnp.sum(total, axis=1, keepdims=True)
    norms[...] = jnp.sum(jnp.where(lane == row, squares, 0.0), axis=0, keepdims=True)


def group_masks(k):
    group = B // k
    row = lax.broadcasted_iota(jnp.int32, (k, B), 0)
    lane = lax.broadcasted_iota(jnp.int32, (k, B), 1)
    return lax.rem(row, group) == lax.div(lane, k), row, lane


def gram_kernel(send, partial_adjoint, norms, *refs):
    arrived, adjoint, packed = refs[:6], refs[6], refs[7]
    k = adjoint.shape[0]
    way = directions()
    for ref, offsets in zip(arrived, received(*way)):
        for i, (a, b) in enumerate(offsets):
            for g in range(ref.shape[1]):
                place = columns(send[0, g, neighbour(-a, -b)])
                adjoint[:, place] += ref[i, g]
    z = adjoint[...]
    gram = lax.dot_general(z, z, BY_LAST, precision=lax.Precision.HIGHEST, preferred_element_type=F32)
    wide = jnp.concatenate([gram, jnp.zeros((k, B - k), F32)], axis=1)
    moved = pltpu.roll(wide, 0, 1, stride=k, stride_axis=0)
    group = B // k
    lines = [jnp.sum(moved[i : i + group], axis=0, keepdims=True) for i in range(0, k, group)]
    lines.append(norms[...])
    lines.append(jnp.zeros(((-len(lines)) % 4, B), F32))
    packed[...] = jnp.broadcast_to(jnp.concatenate(lines, axis=0)[None], packed.shape)


def solve_kernel(count, packed, adjoint, basis_hbm, factor_hbm, gain_hbm, basis, factor, gain, sems):
    k, unknowns = adjoint.shape
    group = B // k
    own, row, lane = group_masks(k)
    sums = jnp.sum(packed[...], axis=0) / count
    gain[...] = sums[k // group : k // group + 1, :k]
    small = [pltpu.make_async_copy(gain, gain_hbm, sems.at[0])]
    small[0].start()
    spread = jnp.concatenate(
        [jnp.broadcast_to(sums[i : i + 1], (group, B)) for i in range(k // group)], axis=0
    )
    gram = jnp.where(own, spread, 0.0)
    shift = k
    while shift < B:
        gram = gram + pltpu.roll(gram, shift, 1)
        shift *= 2
    lines = [jnp.broadcast_to(gram[:, i : i + 1], (k, B)) for i in range(k)]
    both = jnp.where(lane < k, gram, (lane == row + k).astype(F32))
    for i in range(k):
        scale = lax.rsqrt(lines[i][i : i + 1])
        left = lines[i] * scale
        top = both[i : i + 1] * scale
        for j in range(i + 1, k):
            lines[j] = lines[j] - left * left[j : j + 1]
        both = jnp.where(row > i, both - left * top, jnp.where(row == i, top, both))
    factor[...] = jnp.where(lane >= row, both, 0.0)[:, :k]
    small.append(pltpu.make_async_copy(factor, factor_hbm, sems.at[1]))
    small[1].start()
    inverse = both[:, k : 2 * k]
    parts = sems.shape[0] - 2
    copies = []
    for i in range(parts):
        place = pl.ds(i * (unknowns // parts), unknowns // parts)
        basis[:, place] = lax.dot_general(
            inverse,
            adjoint[:, place],
            BY_FIRST,
            precision=lax.Precision.HIGHEST,
            preferred_element_type=F32,
        )
        copies.append(pltpu.make_async_copy(basis.at[:, place], basis_hbm.at[:, place], sems.at[2 + i]))
        copies[-1].start()
    for copy in small + copies:
        copy.wait()


def call(kernel, name, shapes, in_specs, scratch=(), out=VMEM, alias={}, flops=0, bytes_accessed=0):
    return pl.pallas_call(
        kernel,
        name=name,
        out_shape=[jax.ShapeDtypeStruct(shape, dtype) for shape, dtype in shapes],
        in_specs=in_specs,
        out_specs=[out] * len(shapes),
        scratch_shapes=scratch,
        input_output_aliases=alias,
        compiler_params=pltpu.CompilerParams(vmem_limit_bytes=LIMIT),
        cost_estimate=pl.CostEstimate(flops=flops, bytes_accessed=bytes_accessed, transcendentals=0),
    )


def local(blocks, vectors, col_index, row_ptr, send_list):
    k, unknowns = vectors.shape
    rows = unknowns // B
    stored = blocks.shape[0]
    devices = lax.axis_size("dom") * lax.axis_size("sub")
    ghost = send_list.shape[2]
    slots = send_list.shape[1] * ghost
    many = (stored - SHORT * rows) // (LONG - SHORT)
    sizes = (3, 2, 2, 2, 1, 1)
    send_lines = jnp.transpose(send_list, (0, 2, 1))
    inputs = (send_lines, vectors, row_ptr, col_index, blocks)
    here, plan, send, *outgoing = call(
        gather_kernel,
        "gather",
        [(vectors.shape, BF16), ((1, rounded(rows + 1) + rounded(stored)), jnp.int32), (send_lines.shape, jnp.int32)]
        + [((n, ghost, k, B), BF16) for n in sizes],
        [HBM] * 5,
        scratch=[
            pltpu.SMEM(send_lines.shape, jnp.int32),
            pltpu.VMEM(row_ptr.shape, jnp.int32),
            pltpu.VMEM(col_index.shape, jnp.int32),
            pltpu.SemaphoreType.DMA((5,)),
        ],
    )(*[pltpu.with_memory_space_constraint(a, pltpu.HBM) for a in inputs])
    arrived = exchange(*outgoing)
    (partial_image,) = call(
        local_forward_kernel,
        "local_forward",
        [((rows, k, B), F32)],
        [SMEM, VMEM, VMEM],
        flops=2 * rows * LOCAL * B * B * k,
        bytes_accessed=2 * rows * LOCAL * B * B,
    )(plan, here, blocks)
    image, *returns = call(
        ghost_kernel,
        "ghost",
        [((rows, k, B), BF16)] + [((n, ghost, k, B), F32) for n in sizes],
        [SMEM] + [VMEM] * 8,
        scratch=[
            pltpu.VMEM((slots, k, B), BF16),
            pltpu.VMEM((rows, k, B), F32),
            pltpu.VMEM((4, slots, k, B), F32),
            pltpu.SMEM((many + 1,), jnp.int32),
        ],
        flops=4 * (stored - rows * LOCAL) * B * B * k,
        bytes_accessed=4 * (stored - rows * LOCAL) * B * B,
    )(plan, blocks, partial_image, *arrived)
    returned = exchange(*returns)
    partial_adjoint, norms = call(
        local_backward_kernel,
        "local_backward",
        [((k, unknowns), F32), ((1, B), F32)],
        [SMEM, VMEM, VMEM],
        flops=2 * rows * LOCAL * B * B * k,
        bytes_accessed=2 * rows * LOCAL * B * B,
    )(plan, blocks, image)
    adjoint, packed = call(
        gram_kernel,
        "gram",
        [((k, unknowns), F32), ((devices, 4, B), F32)],
        [SMEM] + [VMEM] * 8,
        alias={1: 0},
    )(send, partial_adjoint, norms, *returned)
    everywhere = lax.all_to_all(packed, AXES, 0, 0)
    parts = 4
    basis, factor, gain = call(
        functools.partial(solve_kernel, unknowns * devices),
        "solve",
        [((k, unknowns), F32), ((k, k), F32), ((1, k), F32)],
        [VMEM, VMEM],
        scratch=[
            pltpu.VMEM((k, unknowns), F32),
            pltpu.VMEM((k, k), F32),
            pltpu.VMEM((1, k), F32),
            pltpu.SemaphoreType.DMA((parts + 2,)),
        ],
        out=HBM,
    )(everywhere, adjoint)
    return basis, factor, gain[0]


def solution(mesh):
    return jax.shard_map(
        local,
        mesh=mesh,
        in_specs=(
            P(AXES, None, None),
            P(None, AXES),
            P(AXES, None),
            P(AXES, None),
            P(AXES, None, None),
        ),
        out_specs=(P(None, AXES), P(), P()),
        check_vma=False,
    )
```

```python
import functools

import jax
import jax.numpy as jnp
from jax import lax
from jax.experimental import pallas as pl
from jax.experimental.pallas import tpu as pltpu
from jax.sharding import PartitionSpec as P

AXES = ("dom", "sub")
B = 128
SHORT = 5
LONG = 9
LOCAL = 3
F32 = jnp.float32
BF16 = jnp.bfloat16
BY_LAST = (((1,), (1,)), ((), ()))
BY_FIRST = (((1,), (0,)), ((), ()))
VMEM = pl.BlockSpec(memory_space=pltpu.VMEM)
SMEM = pl.BlockSpec(memory_space=pltpu.SMEM)
ANY = pl.BlockSpec(memory_space=pl.ANY)
HBM = pl.BlockSpec(memory_space=pltpu.HBM)
LIMIT = 8 * 2**20


def neighbour(a, b):
    place = (a + 1) * 3 + b + 1
    return place - (place > 4)


def directions():
    outer, inner = lax.axis_index("dom"), lax.axis_index("sub")
    edge = (inner == 0) | (inner == lax.axis_size("sub") - 1)
    s = 2 * lax.rem(inner, 2) - 1
    u = 1 - 2 * lax.rem(outer, 2)
    return s, u, jnp.where(edge, -u, u)


def columns(block_row):
    return pl.ds(pl.multiple_of(block_row * B, B), B)


def joined(ref, places, axis):
    return jnp.concatenate([ref[place] for place in places], axis=axis)


def sent(s, u, p):
    return (
        ((0, -s), (u, -s), (-u, -s)),
        ((0, s), (p, s)),
        ((-p, s),),
        ((-u, 0),),
        ((u, 0),),
    )


def received(s, u, p):
    return (
        ((0, s),),
        ((0, -s),),
        ((u, -s),),
        ((u, 0), (u, s)),
        ((-u, 0), (-u, s), (-u, -s)),
    )


def exchange(pair, side, cross, far, near):
    n_inner = lax.axis_size("sub")
    devices = lax.axis_size("dom") * n_inner

    def move(array, target):
        return lax.ppermute(array, AXES, [(d, target(d) % devices) for d in range(devices)])

    def step(d):
        return 1 if d % 2 else -1

    def towards(d):
        return n_inner if (d // n_inner) % 2 == 0 else -n_inner

    def beside(d):
        return (d + step(d)) % devices

    pair = move(pair, lambda d: d - step(d))
    side = move(side, beside)
    cross = move(cross, lambda d: beside(d) - towards(beside(d)))
    far = move(jnp.concatenate([far, pair[2:3], far], axis=0), lambda d: d - towards(d))
    near = move(jnp.concatenate([near, pair[1:2], side[1:2]], axis=0), lambda d: d + towards(d))
    return pair, side, cross, far, near


def rounded(size):
    return -(-size // B) * B


def gather_kernel(send_hbm, vectors_hbm, ptr_hbm, col_hbm, blocks_hbm, vectors, plan, send_lines, *refs):
    outgoing, (send, ptr, col, sems) = refs[:5], refs[5:]
    copies = [
        pltpu.make_async_copy(source, target, sems.at[i])
        for i, (source, target) in enumerate(
            (
                (send_hbm, send),
                (vectors_hbm, vectors),
                (ptr_hbm, ptr),
                (col_hbm, col),
                (send_hbm, send_lines),
            )
        )
    ]
    for copy in copies:
        copy.start()
    for copy in copies:
        copy.wait()
    for ref, offsets in zip(outgoing, sent(*directions())):
        for i, (a, b) in enumerate(offsets):
            for g in range(ref.shape[1]):
                ref[i, g] = vectors[:, columns(send[0, g, neighbour(a, b)])]
        for i in range(len(offsets), ref.shape[0]):
            ref[i] = ref[0]
    plan[:, : ptr.shape[1]] = ptr[...]
    plan[:, rounded(ptr.shape[1]) : rounded(ptr.shape[1]) + col.shape[1]] = col[...]


def local_forward_kernel(plan, vectors, blocks, *refs):
    image = refs[-1]
    rows = image.shape[0]
    for j in range(rows):
        e = plan[0, j]
        near = [vectors[:, c * B : c * B + B] for c in (j, (j + 1) % rows, (j - 1) % rows)]
        image[j] = lax.dot_general(
            jnp.concatenate(near, axis=1),
            joined(blocks, [e + t for t in range(LOCAL)], 1),
            BY_LAST,
            preferred_element_type=F32,
        )


def ghost_kernel(plan, blocks, partial_image, *refs):
    arrived, image, outgoing = refs[:5], refs[5], refs[6:11]
    ghosts, total, spread, long_rows = refs[11:]
    rows = image.shape[0]
    many = long_rows.shape[0] - 1
    first_column = rounded(rows + 1)
    way = directions()
    for ref, offsets in zip(arrived, received(*way)):
        for i, (a, b) in enumerate(offsets):
            for g in range(ref.shape[1]):
                ghosts[neighbour(a, b) * ref.shape[1] + g] = ref[i, g]
    found = 0
    for j in range(rows):
        long_rows[jnp.minimum(found, many)] = j
        found = found + (plan[0, j + 1] - plan[0, j] > SHORT).astype(jnp.int32)

    def forward(e, first, last):
        return lax.dot_general(
            joined(ghosts, [plan[0, first_column + e + t] - rows for t in range(first, last)], 1),
            joined(blocks, [e + t for t in range(first, last)], 1),
            BY_LAST,
            preferred_element_type=F32,
        )

    for j in range(rows):
        total[j] = partial_image[j] + forward(plan[0, j], LOCAL, SHORT)
    for i in range(many):
        j = long_rows[i]
        total[j] += forward(plan[0, j], SHORT, LONG)
    image[...] = total[...].astype(BF16)
    spread[...] = jnp.zeros_like(spread)
    banks = spread.shape[0]

    def backward(j, first, last):
        e = plan[0, j]
        terms = lax.dot_general(
            image[j],
            joined(blocks, [e + t for t in range(first, last)], 1),
            BY_FIRST,
            preferred_element_type=F32,
        )
        for t in range(first, last):
            k = t - first
            spread[k % banks, plan[0, first_column + e + t] - rows] += terms[:, k * B : k * B + B]

    for j in range(rows):
        backward(j, LOCAL, SHORT)
    for i in range(many):
        backward(long_rows[i], SHORT, LONG)
    for ref, offsets in zip(outgoing, sent(*way)):
        for i, (a, b) in enumerate(offsets):
            for g in range(ref.shape[1]):
                slot = neighbour(-a, -b) * ref.shape[1] + g
                ref[i, g] = sum(spread[bank, slot] for bank in range(banks))
        for i in range(len(offsets), ref.shape[0]):
            ref[i] = ref[0]


def local_backward_kernel(plan, blocks, image, adjoint, norms):
    rows, k = image.shape[:2]
    total = jnp.zeros((k, B), F32)
    for j in range(rows):
        before, after = (j - 1) % rows, (j + 1) % rows
        adjoint[:, j * B : j * B + B] = lax.dot_general(
            joined(image, [j, before, after], 1),
            joined(blocks, [plan[0, j], plan[0, before] + 1, plan[0, after] + 2], 0),
            BY_FIRST,
            preferred_element_type=F32,
        )
        wide = image[j].astype(F32)
        total = total + wide * wide
    row = lax.broadcasted_iota(jnp.int32, (k, B), 0)
    lane = lax.broadcasted_iota(jnp.int32, (k, B), 1)
    squares = jnp.sum(total, axis=1, keepdims=True)
    norms[...] = jnp.sum(jnp.where(lane == row, squares, 0.0), axis=0, keepdims=True)


def group_masks(k):
    group = B // k
    row = lax.broadcasted_iota(jnp.int32, (k, B), 0)
    lane = lax.broadcasted_iota(jnp.int32, (k, B), 1)
    return lax.rem(row, group) == lax.div(lane, k), row, lane


def gram_kernel(send, partial_adjoint, norms, *refs):
    arrived, adjoint, packed = refs[:5], refs[5], refs[6]
    k = adjoint.shape[0]
    way = directions()
    for ref, offsets in zip(arrived, received(*way)):
        for i, (a, b) in enumerate(offsets):
            for g in range(ref.shape[1]):
                place = columns(send[0, g, neighbour(-a, -b)])
                adjoint[:, place] += ref[i, g]
    z = adjoint[...]
    gram = lax.dot_general(z, z, BY_LAST, precision=lax.Precision.HIGHEST, preferred_element_type=F32)
    wide = jnp.concatenate([gram, jnp.zeros((k, B - k), F32)], axis=1)
    moved = pltpu.roll(wide, 0, 1, stride=k, stride_axis=0)
    group = B // k
    lines = [jnp.sum(moved[i : i + group], axis=0, keepdims=True) for i in range(0, k, group)]
    lines.append(norms[...])
    lines.append(jnp.zeros(((-len(lines)) % 4, B), F32))
    packed[...] = jnp.broadcast_to(jnp.concatenate(lines, axis=0)[None], packed.shape)


def solve_kernel(count, packed, adjoint, basis_hbm, factor_hbm, gain_hbm, basis, factor, gain, sems):
    k, unknowns = adjoint.shape
    group = B // k
    own, row, lane = group_masks(k)
    sums = jnp.sum(packed[...], axis=0) / count
    gain[...] = sums[k // group : k // group + 1, :k]
    small = [pltpu.make_async_copy(gain, gain_hbm, sems.at[0])]
    small[0].start()
    spread = jnp.concatenate(
        [jnp.broadcast_to(sums[i : i + 1], (group, B)) for i in range(k // group)], axis=0
    )
    gram = jnp.where(own, spread, 0.0)
    shift = k
    while shift < B:
        gram = gram + pltpu.roll(gram, shift, 1)
        shift *= 2
    lines = [jnp.broadcast_to(gram[:, i : i + 1], (k, B)) for i in range(k)]
    both = jnp.where(lane < k, gram, (lane == row + k).astype(F32))
    for i in range(k):
        scale = lax.rsqrt(lines[i][i : i + 1])
        left = lines[i] * scale
        top = both[i : i + 1] * scale
        for j in range(i + 1, k):
            lines[j] = lines[j] - left * left[j : j + 1]
        both = jnp.where(row > i, both - left * top, jnp.where(row == i, top, both))
    factor[...] = jnp.where(lane >= row, both, 0.0)[:, :k]
    small.append(pltpu.make_async_copy(factor, factor_hbm, sems.at[1]))
    small[1].start()
    inverse = both[:, k : 2 * k]
    parts = sems.shape[0] - 2
    copies = []
    for i in range(parts):
        place = pl.ds(i * (unknowns // parts), unknowns // parts)
        basis[:, place] = lax.dot_general(
            inverse,
            adjoint[:, place],
            BY_FIRST,
            precision=lax.Precision.HIGHEST,
            preferred_element_type=F32,
        )
        copies.append(pltpu.make_async_copy(basis.at[:, place], basis_hbm.at[:, place], sems.at[2 + i]))
        copies[-1].start()
    for copy in small + copies:
        copy.wait()


def call(kernel, name, shapes, in_specs, scratch=(), out=VMEM, alias={}, flops=0, bytes_accessed=0):
    return pl.pallas_call(
        kernel,
        name=name,
        out_shape=[jax.ShapeDtypeStruct(shape, dtype) for shape, dtype in shapes],
        in_specs=in_specs,
        out_specs=[out] * len(shapes),
        scratch_shapes=scratch,
        input_output_aliases=alias,
        compiler_params=pltpu.CompilerParams(vmem_limit_bytes=LIMIT),
        cost_estimate=pl.CostEstimate(flops=flops, bytes_accessed=bytes_accessed, transcendentals=0),
    )


def local(blocks, vectors, col_index, row_ptr, send_list):
    k, unknowns = vectors.shape
    rows = unknowns // B
    stored = blocks.shape[0]
    devices = lax.axis_size("dom") * lax.axis_size("sub")
    ghost = send_list.shape[2]
    slots = send_list.shape[1] * ghost
    many = (stored - SHORT * rows) // (LONG - SHORT)
    sizes = (3, 3, 4, 1, 1)
    send_lines = jnp.transpose(send_list, (0, 2, 1))
    inputs = (send_lines, vectors, row_ptr, col_index, blocks)
    here, plan, send, *outgoing = call(
        gather_kernel,
        "gather",
        [(vectors.shape, BF16), ((1, rounded(rows + 1) + rounded(stored)), jnp.int32), (send_lines.shape, jnp.int32)]
        + [((n, ghost, k, B), BF16) for n in sizes],
        [HBM] * 5,
        scratch=[
            pltpu.SMEM(send_lines.shape, jnp.int32),
            pltpu.VMEM(row_ptr.shape, jnp.int32),
            pltpu.VMEM(col_index.shape, jnp.int32),
            pltpu.SemaphoreType.DMA((5,)),
        ],
    )(*[pltpu.with_memory_space_constraint(a, pltpu.HBM) for a in inputs])
    arrived = exchange(*outgoing)
    (partial_image,) = call(
        local_forward_kernel,
        "local_forward",
        [((rows, k, B), F32)],
        [SMEM, VMEM, VMEM],
        flops=2 * rows * LOCAL * B * B * k,
        bytes_accessed=2 * rows * LOCAL * B * B,
    )(plan, here, blocks)
    image, *returns = call(
        ghost_kernel,
        "ghost",
        [((rows, k, B), BF16)] + [((n, ghost, k, B), F32) for n in sizes],
        [SMEM] + [VMEM] * 7,
        scratch=[
            pltpu.VMEM((slots, k, B), BF16),
            pltpu.VMEM((rows, k, B), F32),
            pltpu.VMEM((4, slots, k, B), F32),
            pltpu.SMEM((many + 1,), jnp.int32),
        ],
        flops=4 * (stored - rows * LOCAL) * B * B * k,
        bytes_accessed=4 * (stored - rows * LOCAL) * B * B,
    )(plan, blocks, partial_image, *arrived)
    returned = exchange(*returns)
    partial_adjoint, norms = call(
        local_backward_kernel,
        "local_backward",
        [((k, unknowns), F32), ((1, B), F32)],
        [SMEM, VMEM, VMEM],
        flops=2 * rows * LOCAL * B * B * k,
        bytes_accessed=2 * rows * LOCAL * B * B,
    )(plan, blocks, image)
    adjoint, packed = call(
        gram_kernel,
        "gram",
        [((k, unknowns), F32), ((devices, 4, B), F32)],
        [SMEM] + [VMEM] * 7,
        alias={1: 0},
    )(send, partial_adjoint, norms, *returned)
    everywhere = lax.all_to_all(packed, AXES, 0, 0)
    parts = 4
    basis, factor, gain = call(
        functools.partial(solve_kernel, unknowns * devices),
        "solve",
        [((k, unknowns), F32), ((k, k), F32), ((1, k), F32)],
        [VMEM, VMEM],
        scratch=[
            pltpu.VMEM((k, unknowns), F32),
            pltpu.VMEM((k, k), F32),
            pltpu.VMEM((1, k), F32),
            pltpu.SemaphoreType.DMA((parts + 2,)),
        ],
        out=HBM,
    )(everywhere, adjoint)
    return basis, factor, gain[0]


def solution(mesh):
    return jax.shard_map(
        local,
        mesh=mesh,
        in_specs=(
            P(AXES, None, None),
            P(None, AXES),
            P(AXES, None),
            P(AXES, None),
            P(AXES, None, None),
        ),
        out_specs=(P(None, AXES), P(), P()),
        check_vma=False,
    )
```

```python
import functools

import jax
import jax.numpy as jnp
from jax import lax
from jax.experimental import pallas as pl
from jax.experimental.pallas import tpu as pltpu
from jax.sharding import PartitionSpec as P

AXES = ("dom", "sub")
B = 128
SHORT = 5
LONG = 9
LOCAL = 3
F32 = jnp.float32
BF16 = jnp.bfloat16
BY_LAST = (((1,), (1,)), ((), ()))
BY_FIRST = (((1,), (0,)), ((), ()))
VMEM = pl.BlockSpec(memory_space=pltpu.VMEM)
SMEM = pl.BlockSpec(memory_space=pltpu.SMEM)
ANY = pl.BlockSpec(memory_space=pl.ANY)
HBM = pl.BlockSpec(memory_space=pltpu.HBM)
LIMIT = 8 * 2**20


def neighbour(a, b):
    place = (a + 1) * 3 + b + 1
    return place - (place > 4)


def directions():
    outer, inner = lax.axis_index("dom"), lax.axis_index("sub")
    edge = (inner == 0) | (inner == lax.axis_size("sub") - 1)
    s = 2 * lax.rem(inner, 2) - 1
    u = 1 - 2 * lax.rem(outer, 2)
    return s, u, jnp.where(edge, -u, u)


def columns(block_row):
    return pl.ds(pl.multiple_of(block_row * B, B), B)


def joined(ref, places, axis):
    return jnp.concatenate([ref[place] for place in places], axis=axis)


def sent(s, u, p):
    return (
        ((0, -s), (u, -s), (-u, -s)),
        ((0, s), (p, s)),
        ((-p, s),),
        ((-u, 0),),
        ((u, 0),),
    )


def received(s, u, p):
    return (
        ((0, s),),
        ((0, -s),),
        ((u, -s),),
        ((u, 0), (u, s)),
        ((-u, 0), (-u, s), (-u, -s)),
    )


def exchange(pair, side, cross, far, near):
    n_inner = lax.axis_size("sub")
    devices = lax.axis_size("dom") * n_inner

    def move(array, target):
        return lax.ppermute(array, AXES, [(d, target(d) % devices) for d in range(devices)])

    def step(d):
        return 1 if d % 2 else -1

    def towards(d):
        return n_inner if (d // n_inner) % 2 == 0 else -n_inner

    def beside(d):
        return (d + step(d)) % devices

    pair = move(pair, lambda d: d - step(d))
    side = move(side, beside)
    cross = move(cross, lambda d: beside(d) - towards(beside(d)))
    far = move(jnp.concatenate([far, pair[2:3], far], axis=0), lambda d: d - towards(d))
    near = move(jnp.concatenate([near, pair[1:2], side[1:2]], axis=0), lambda d: d + towards(d))
    return pair, side, cross, far, near


def rounded(size):
    return -(-size // B) * B


def gather_kernel(send_hbm, vectors_hbm, ptr_hbm, col_hbm, blocks_hbm, vectors, plan, send_lines, *refs):
    outgoing, (send, ptr, col, sems) = refs[:5], refs[5:]
    copies = [
        pltpu.make_async_copy(source, target, sems.at[i])
        for i, (source, target) in enumerate(
            (
                (send_hbm, send),
                (vectors_hbm, vectors),
                (ptr_hbm, ptr),
                (col_hbm, col),
                (send_hbm, send_lines),
            )
        )
    ]
    for copy in copies:
        copy.start()
    for copy in copies:
        copy.wait()
    for ref, offsets in zip(outgoing, sent(*directions())):
        for i, (a, b) in enumerate(offsets):
            for g in range(ref.shape[1]):
                ref[i, g] = vectors[:, columns(send[0, g, neighbour(a, b)])]
        for i in range(len(offsets), ref.shape[0]):
            ref[i] = ref[0]
    plan[:, : ptr.shape[1]] = ptr[...]
    plan[:, rounded(ptr.shape[1]) : rounded(ptr.shape[1]) + col.shape[1]] = col[...]


def local_forward_kernel(plan, vectors, blocks, *refs):
    image = refs[-1]
    rows = image.shape[0]
    for j in range(rows):
        e = plan[0, j]
        near = [vectors[:, c * B : c * B + B] for c in (j, (j + 1) % rows, (j - 1) % rows)]
        image[j] = lax.dot_general(
            jnp.concatenate(near, axis=1),
            joined(blocks, [e + t for t in range(LOCAL)], 1),
            BY_LAST,
            preferred_element_type=F32,
        )


def ghost_kernel(plan, blocks, partial_image, *refs):
    arrived, image, outgoing = refs[:5], refs[5], refs[6:11]
    ghosts, total, spread, long_rows = refs[11:]
    rows = image.shape[0]
    many = long_rows.shape[0] - 1
    first_column = rounded(rows + 1)
    way = directions()
    for ref, offsets in zip(arrived, received(*way)):
        for i, (a, b) in enumerate(offsets):
            for g in range(ref.shape[1]):
                ghosts[neighbour(a, b) * ref.shape[1] + g] = ref[i, g]
    found = 0
    for j in range(rows):
        long_rows[jnp.minimum(found, many)] = j
        found = found + (plan[0, j + 1] - plan[0, j] > SHORT).astype(jnp.int32)

    def forward(e, first, last):
        return lax.dot_general(
            joined(ghosts, [plan[0, first_column + e + t] - rows for t in range(first, last)], 1),
            joined(blocks, [e + t for t in range(first, last)], 1),
            BY_LAST,
            preferred_element_type=F32,
        )

    for j in range(rows):
        total[j] = partial_image[j] + forward(plan[0, j], LOCAL, SHORT)
    for i in range(many):
        j = long_rows[i]
        total[j] += forward(plan[0, j], SHORT, LONG)
    image[...] = total[...].astype(BF16)
    spread[...] = jnp.zeros_like(spread)
    banks = spread.shape[0]

    def backward(j, first, last):
        e = plan[0, j]
        terms = lax.dot_general(
            image[j],
            joined(blocks, [e + t for t in range(first, last)], 1),
            BY_FIRST,
            preferred_element_type=F32,
        )
        for t in range(first, last):
            k = t - first
            spread[k % banks, plan[0, first_column + e + t] - rows] += terms[:, k * B : k * B + B]

    for j in range(rows):
        backward(j, LOCAL, SHORT)
    for i in range(many):
        backward(long_rows[i], SHORT, LONG)
    for ref, offsets in zip(outgoing, sent(*way)):
        for i, (a, b) in enumerate(offsets):
            for g in range(ref.shape[1]):
                slot = neighbour(-a, -b) * ref.shape[1] + g
                ref[i, g] = sum(spread[bank, slot] for bank in range(banks))
        for i in range(len(offsets), ref.shape[0]):
            ref[i] = ref[0]


def local_backward_kernel(plan, blocks, image, adjoint, norms):
    rows, k = image.shape[:2]
    total = jnp.zeros((k, B), F32)
    for j in range(rows):
        before, after = (j - 1) % rows, (j + 1) % rows
        adjoint[:, j * B : j * B + B] = lax.dot_general(
            joined(image, [j, before, after], 1),
            joined(blocks, [plan[0, j], plan[0, before] + 1, plan[0, after] + 2], 0),
            BY_FIRST,
            preferred_element_type=F32,
        )
        wide = image[j].astype(F32)
        total = total + wide * wide
    row = lax.broadcasted_iota(jnp.int32, (k, B), 0)
    lane = lax.broadcasted_iota(jnp.int32, (k, B), 1)
    squares = jnp.sum(total, axis=1, keepdims=True)
    norms[...] = jnp.sum(jnp.where(lane == row, squares, 0.0), axis=0, keepdims=True)


def group_masks(k):
    group = B // k
    row = lax.broadcasted_iota(jnp.int32, (k, B), 0)
    lane = lax.broadcasted_iota(jnp.int32, (k, B), 1)
    return lax.rem(row, group) == lax.div(lane, k), row, lane


def gram_kernel(send, partial_adjoint, norms, *refs):
    arrived, adjoint, packed = refs[:5], refs[5], refs[6]
    k = adjoint.shape[0]
    way = directions()
    for ref, offsets in zip(arrived, received(*way)):
        for i, (a, b) in enumerate(offsets):
            for g in range(ref.shape[1]):
                place = columns(send[0, g, neighbour(-a, -b)])
                adjoint[:, place] += ref[i, g]
    z = adjoint[...]
    gram = lax.dot_general(z, z, BY_LAST, precision=lax.Precision.HIGHEST, preferred_element_type=F32)
    wide = jnp.concatenate([gram, jnp.zeros((k, B - k), F32)], axis=1)
    moved = pltpu.roll(wide, 0, 1, stride=k, stride_axis=0)
    group = B // k
    lines = [jnp.sum(moved[i : i + group], axis=0, keepdims=True) for i in range(0, k, group)]
    lines.append(norms[...])
    lines.append(jnp.zeros(((-len(lines)) % 4, B), F32))
    packed[...] = jnp.broadcast_to(jnp.concatenate(lines, axis=0)[None], packed.shape)


def solve_kernel(count, packed, adjoint, basis_hbm, factor_hbm, gain_hbm, basis, factor, gain, sems):
    k, unknowns = adjoint.shape
    group = B // k
    own, row, lane = group_masks(k)
    sums = jnp.sum(packed[...], axis=0) / count
    gain[...] = sums[k // group : k // group + 1, :k]
    small = [pltpu.make_async_copy(gain, gain_hbm, sems.at[0])]
    small[0].start()
    spread = jnp.concatenate(
        [jnp.broadcast_to(sums[i : i + 1], (group, B)) for i in range(k // group)], axis=0
    )
    gram = jnp.where(own, spread, 0.0)
    shift = k
    while shift < B:
        gram = gram + pltpu.roll(gram, shift, 1)
        shift *= 2
    lines = [jnp.broadcast_to(gram[:, i : i + 1], (k, B)) for i in range(k)]
    both = jnp.where(lane < k, gram, (lane == row + k).astype(F32))
    for i in range(k):
        scale = lax.rsqrt(lines[i][i : i + 1])
        left = lines[i] * scale
        top = both[i : i + 1] * scale
        for j in range(i + 1, k):
            lines[j] = lines[j] - left * left[j : j + 1]
        both = jnp.where(row > i, both - left * top, jnp.where(row == i, top, both))
    factor[...] = jnp.where(lane >= row, both, 0.0)[:, :k]
    small.append(pltpu.make_async_copy(factor, factor_hbm, sems.at[1]))
    small[1].start()
    inverse = both[:, k : 2 * k]
    parts = sems.shape[0] - 2
    copies = []
    for i in range(parts):
        place = pl.ds(i * (unknowns // parts), unknowns // parts)
        basis[:, place] = lax.dot_general(
            inverse,
            adjoint[:, place],
            BY_FIRST,
            precision=lax.Precision.HIGHEST,
            preferred_element_type=F32,
        )
        copies.append(pltpu.make_async_copy(basis.at[:, place], basis_hbm.at[:, place], sems.at[2 + i]))
        copies[-1].start()
    for copy in small + copies:
        copy.wait()


def call(kernel, name, shapes, in_specs, scratch=(), out=VMEM, alias={}, flops=0, bytes_accessed=0):
    return pl.pallas_call(
        kernel,
        name=name,
        out_shape=[jax.ShapeDtypeStruct(shape, dtype) for shape, dtype in shapes],
        in_specs=in_specs,
        out_specs=[out] * len(shapes),
        scratch_shapes=scratch,
        input_output_aliases=alias,
        compiler_params=pltpu.CompilerParams(vmem_limit_bytes=LIMIT),
        cost_estimate=pl.CostEstimate(flops=flops, bytes_accessed=bytes_accessed, transcendentals=0),
    )


def local(blocks, vectors, col_index, row_ptr, send_list):
    k, unknowns = vectors.shape
    rows = unknowns // B
    stored = blocks.shape[0]
    devices = lax.axis_size("dom") * lax.axis_size("sub")
    ghost = send_list.shape[2]
    slots = send_list.shape[1] * ghost
    many = (stored - SHORT * rows) // (LONG - SHORT)
    sizes = (3, 3, 3, 1, 1)
    send_lines = jnp.transpose(send_list, (0, 2, 1))
    inputs = (send_lines, vectors, row_ptr, col_index, blocks)
    here, plan, send, *outgoing = call(
        gather_kernel,
        "gather",
        [(vectors.shape, BF16), ((1, rounded(rows + 1) + rounded(stored)), jnp.int32), (send_lines.shape, jnp.int32)]
        + [((n, ghost, k, B), BF16) for n in sizes],
        [HBM] * 5,
        scratch=[
            pltpu.SMEM(send_lines.shape, jnp.int32),
            pltpu.VMEM(row_ptr.shape, jnp.int32),
            pltpu.VMEM(col_index.shape, jnp.int32),
            pltpu.SemaphoreType.DMA((5,)),
        ],
    )(*[pltpu.with_memory_space_constraint(a, pltpu.HBM) for a in inputs])
    arrived = exchange(*outgoing)
    (partial_image,) = call(
        local_forward_kernel,
        "local_forward",
        [((rows, k, B), F32)],
        [SMEM, VMEM, VMEM],
        flops=2 * rows * LOCAL * B * B * k,
        bytes_accessed=2 * rows * LOCAL * B * B,
    )(plan, here, blocks)
    image, *returns = call(
        ghost_kernel,
        "ghost",
        [((rows, k, B), BF16)] + [((n, ghost, k, B), F32) for n in sizes],
        [SMEM] + [VMEM] * 7,
        scratch=[
            pltpu.VMEM((slots, k, B), BF16),
            pltpu.VMEM((rows, k, B), F32),
            pltpu.VMEM((4, slots, k, B), F32),
            pltpu.SMEM((many + 1,), jnp.int32),
        ],
        flops=4 * (stored - rows * LOCAL) * B * B * k,
        bytes_accessed=4 * (stored - rows * LOCAL) * B * B,
    )(plan, blocks, partial_image, *arrived)
    returned = exchange(*returns)
    partial_adjoint, norms = call(
        local_backward_kernel,
        "local_backward",
        [((k, unknowns), F32), ((1, B), F32)],
        [SMEM, VMEM, VMEM],
        flops=2 * rows * LOCAL * B * B * k,
        bytes_accessed=2 * rows * LOCAL * B * B,
    )(plan, blocks, image)
    adjoint, packed = call(
        gram_kernel,
        "gram",
        [((k, unknowns), F32), ((devices, 4, B), F32)],
        [SMEM] + [VMEM] * 7,
        alias={1: 0},
    )(send, partial_adjoint, norms, *returned)
    everywhere = lax.all_to_all(packed, AXES, 0, 0)
    parts = 4
    basis, factor, gain = call(
        functools.partial(solve_kernel, unknowns * devices),
        "solve",
        [((k, unknowns), F32), ((k, k), F32), ((1, k), F32)],
        [VMEM, VMEM],
        scratch=[
            pltpu.VMEM((k, unknowns), F32),
            pltpu.VMEM((k, k), F32),
            pltpu.VMEM((1, k), F32),
            pltpu.SemaphoreType.DMA((parts + 2,)),
        ],
        out=HBM,
    )(everywhere, adjoint)
    return basis, factor, gain[0]


def solution(mesh):
    return jax.shard_map(
        local,
        mesh=mesh,
        in_specs=(
            P(AXES, None, None),
            P(None, AXES),
            P(AXES, None),
            P(AXES, None),
            P(AXES, None, None),
        ),
        out_specs=(P(None, AXES), P(), P()),
        check_vma=False,
    )
```

```python
import functools

import jax
import jax.numpy as jnp
from jax import lax
from jax.experimental import pallas as pl
from jax.experimental.pallas import tpu as pltpu
from jax.sharding import PartitionSpec as P

AXES = ("dom", "sub")
B = 128
SHORT = 5
LONG = 9
LOCAL = 3
F32 = jnp.float32
BF16 = jnp.bfloat16
BY_LAST = (((1,), (1,)), ((), ()))
BY_FIRST = (((1,), (0,)), ((), ()))
VMEM = pl.BlockSpec(memory_space=pltpu.VMEM)
SMEM = pl.BlockSpec(memory_space=pltpu.SMEM)
ANY = pl.BlockSpec(memory_space=pl.ANY)
HBM = pl.BlockSpec(memory_space=pltpu.HBM)
LIMIT = 8 * 2**20


def neighbour(a, b):
    place = (a + 1) * 3 + b + 1
    return place - (place > 4)


def directions():
    outer, inner = lax.axis_index("dom"), lax.axis_index("sub")
    edge = (inner == 0) | (inner == lax.axis_size("sub") - 1)
    s = 2 * lax.rem(inner, 2) - 1
    u = 1 - 2 * lax.rem(outer, 2)
    return s, u, jnp.where(edge, -u, u)


def columns(block_row):
    return pl.ds(pl.multiple_of(block_row * B, B), B)


def joined(ref, places, axis):
    return jnp.concatenate([ref[place] for place in places], axis=axis)


def sent(s, u, p):
    return (
        ((0, -s), (u, -s), (-u, -s)),
        ((0, s), (p, s)),
        ((-p, s),),
        ((-u, 0),),
        ((u, 0),),
    )


def received(s, u, p):
    return (
        ((0, s),),
        ((0, -s),),
        ((u, -s),),
        ((u, 0), (u, s)),
        ((-u, 0), (-u, s), (-u, -s)),
    )


def exchange(pair, side, cross, far, near):
    n_inner = lax.axis_size("sub")
    devices = lax.axis_size("dom") * n_inner

    def move(array, target):
        return lax.ppermute(array, AXES, [(d, target(d) % devices) for d in range(devices)])

    def step(d):
        return 1 if d % 2 else -1

    def towards(d):
        return n_inner if (d // n_inner) % 2 == 0 else -n_inner

    def beside(d):
        return (d + step(d)) % devices

    pair = move(pair, lambda d: d - step(d))
    side = move(side, beside)
    cross = move(cross, lambda d: beside(d) - towards(beside(d)))
    far = move(jnp.concatenate([far, pair[2:3], far], axis=0), lambda d: d - towards(d))
    near = move(jnp.concatenate([near, pair[1:2], side[1:2]], axis=0), lambda d: d + towards(d))
    return pair, side, cross, far, near


def rounded(size):
    return -(-size // B) * B


def gather_kernel(send_hbm, vectors_hbm, ptr_hbm, col_hbm, blocks_hbm, vectors, plan, send_lines, *refs):
    outgoing, (send, ptr, col, sems) = refs[:5], refs[5:]
    copies = [
        pltpu.make_async_copy(source, target, sems.at[i])
        for i, (source, target) in enumerate(
            (
                (send_hbm, send),
                (vectors_hbm, vectors),
                (ptr_hbm, ptr),
                (col_hbm, col),
                (send_hbm, send_lines),
            )
        )
    ]
    for copy in copies:
        copy.start()
    for copy in copies:
        copy.wait()
    for ref, offsets in zip(outgoing, sent(*directions())):
        for i, (a, b) in enumerate(offsets):
            for g in range(ref.shape[1]):
                ref[i, g] = vectors[:, columns(send[0, g, neighbour(a, b)])]
        for i in range(len(offsets), ref.shape[0]):
            ref[i] = ref[0]
    plan[:, : ptr.shape[1]] = ptr[...]
    plan[:, rounded(ptr.shape[1]) : rounded(ptr.shape[1]) + col.shape[1]] = col[...]


def local_forward_kernel(plan, vectors, blocks, *refs):
    image = refs[-1]
    rows = image.shape[0]
    for j in range(rows):
        e = plan[0, j]
        near = [vectors[:, c * B : c * B + B] for c in (j, (j + 1) % rows, (j - 1) % rows)]
        image[j] = lax.dot_general(
            jnp.concatenate(near, axis=1),
            joined(blocks, [e + t for t in range(LOCAL)], 1),
            BY_LAST,
            preferred_element_type=F32,
        )


def ghost_kernel(plan_lines, blocks, partial_image, *refs):
    arrived, image, outgoing = refs[:5], refs[5], refs[6:11]
    ghosts, total, spread, long_rows, plan, sem = refs[11:]
    load = pltpu.make_async_copy(plan_lines, plan, sem)
    load.start()
    spread[...] = jnp.zeros_like(spread)
    rows = image.shape[0]
    many = long_rows.shape[0] - 1
    first_column = rounded(rows + 1)
    way = directions()
    for ref, offsets in zip(arrived, received(*way)):
        for i, (a, b) in enumerate(offsets):
            for g in range(ref.shape[1]):
                ghosts[neighbour(a, b) * ref.shape[1] + g] = ref[i, g]
    load.wait()
    found = 0
    for j in range(rows):
        long_rows[jnp.minimum(found, many)] = j
        found = found + (plan[0, j + 1] - plan[0, j] > SHORT).astype(jnp.int32)

    def forward(e, first, last):
        return lax.dot_general(
            joined(ghosts, [plan[0, first_column + e + t] - rows for t in range(first, last)], 1),
            joined(blocks, [e + t for t in range(first, last)], 1),
            BY_LAST,
            preferred_element_type=F32,
        )

    for j in range(rows):
        total[j] = partial_image[j] + forward(plan[0, j], LOCAL, SHORT)
    for i in range(many):
        j = long_rows[i]
        total[j] += forward(plan[0, j], SHORT, LONG)
    image[...] = total[...].astype(BF16)
    banks = spread.shape[0]

    def backward(j, first, last):
        e = plan[0, j]
        terms = lax.dot_general(
            image[j],
            joined(blocks, [e + t for t in range(first, last)], 1),
            BY_FIRST,
            preferred_element_type=F32,
        )
        for t in range(first, last):
            k = t - first
            spread[k % banks, plan[0, first_column + e + t] - rows] += terms[:, k * B : k * B + B]

    for j in range(rows):
        backward(j, LOCAL, SHORT)
    for i in range(many):
        backward(long_rows[i], SHORT, LONG)
    for ref, offsets in zip(outgoing, sent(*way)):
        for i, (a, b) in enumerate(offsets):
            for g in range(ref.shape[1]):
                slot = neighbour(-a, -b) * ref.shape[1] + g
                ref[i, g] = sum(spread[bank, slot] for bank in range(banks))
        for i in range(len(offsets), ref.shape[0]):
            ref[i] = ref[0]


def local_backward_kernel(plan, blocks, image, adjoint, norms):
    rows, k = image.shape[:2]
    total = jnp.zeros((k, B), F32)
    for j in range(rows):
        before, after = (j - 1) % rows, (j + 1) % rows
        adjoint[:, j * B : j * B + B] = lax.dot_general(
            joined(image, [j, before, after], 1),
            joined(blocks, [plan[0, j], plan[0, before] + 1, plan[0, after] + 2], 0),
            BY_FIRST,
            preferred_element_type=F32,
        )
        wide = image[j].astype(F32)
        total = total + wide * wide
    row = lax.broadcasted_iota(jnp.int32, (k, B), 0)
    lane = lax.broadcasted_iota(jnp.int32, (k, B), 1)
    squares = jnp.sum(total, axis=1, keepdims=True)
    norms[...] = jnp.sum(jnp.where(lane == row, squares, 0.0), axis=0, keepdims=True)


def group_masks(k):
    group = B // k
    row = lax.broadcasted_iota(jnp.int32, (k, B), 0)
    lane = lax.broadcasted_iota(jnp.int32, (k, B), 1)
    return lax.rem(row, group) == lax.div(lane, k), row, lane


def gram_kernel(send, partial_adjoint, norms, *refs):
    arrived, adjoint, packed = refs[:5], refs[5], refs[6]
    k = adjoint.shape[0]
    way = directions()
    for ref, offsets in zip(arrived, received(*way)):
        for i, (a, b) in enumerate(offsets):
            for g in range(ref.shape[1]):
                place = columns(send[0, g, neighbour(-a, -b)])
                adjoint[:, place] += ref[i, g]
    z = adjoint[...]
    gram = lax.dot_general(z, z, BY_LAST, precision=lax.Precision.HIGHEST, preferred_element_type=F32)
    wide = jnp.concatenate([gram, jnp.zeros((k, B - k), F32)], axis=1)
    moved = pltpu.roll(wide, 0, 1, stride=k, stride_axis=0)
    group = B // k
    lines = [jnp.sum(moved[i : i + group], axis=0, keepdims=True) for i in range(0, k, group)]
    lines.append(norms[...])
    lines.append(jnp.zeros(((-len(lines)) % 4, B), F32))
    packed[...] = jnp.broadcast_to(jnp.concatenate(lines, axis=0)[None], packed.shape)


def solve_kernel(count, packed, adjoint, basis_hbm, factor_hbm, gain_hbm, basis, factor, gain, sems):
    k, unknowns = adjoint.shape
    group = B // k
    own, row, lane = group_masks(k)
    sums = jnp.sum(packed[...], axis=0) / count
    gain[...] = sums[k // group : k // group + 1, :k]
    small = [pltpu.make_async_copy(gain, gain_hbm, sems.at[0])]
    small[0].start()
    spread = jnp.concatenate(
        [jnp.broadcast_to(sums[i : i + 1], (group, B)) for i in range(k // group)], axis=0
    )
    gram = jnp.where(own, spread, 0.0)
    shift = k
    while shift < B:
        gram = gram + pltpu.roll(gram, shift, 1)
        shift *= 2
    lines = [jnp.broadcast_to(gram[:, i : i + 1], (k, B)) for i in range(k)]
    both = jnp.where(lane < k, gram, (lane == row + k).astype(F32))
    for i in range(k):
        scale = lax.rsqrt(lines[i][i : i + 1])
        left = lines[i] * scale
        top = both[i : i + 1] * scale
        for j in range(i + 1, k):
            lines[j] = lines[j] - left * left[j : j + 1]
        both = jnp.where(row > i, both - left * top, jnp.where(row == i, top, both))
    factor[...] = jnp.where(lane >= row, both, 0.0)[:, :k]
    small.append(pltpu.make_async_copy(factor, factor_hbm, sems.at[1]))
    small[1].start()
    inverse = both[:, k : 2 * k]
    parts = sems.shape[0] - 2
    copies = []
    for i in range(parts):
        place = pl.ds(i * (unknowns // parts), unknowns // parts)
        basis[:, place] = lax.dot_general(
            inverse,
            adjoint[:, place],
            BY_FIRST,
            precision=lax.Precision.HIGHEST,
            preferred_element_type=F32,
        )
        copies.append(pltpu.make_async_copy(basis.at[:, place], basis_hbm.at[:, place], sems.at[2 + i]))
        copies[-1].start()
    for copy in small + copies:
        copy.wait()


def call(kernel, name, shapes, in_specs, scratch=(), out=VMEM, alias={}, flops=0, bytes_accessed=0):
    return pl.pallas_call(
        kernel,
        name=name,
        out_shape=[jax.ShapeDtypeStruct(shape, dtype) for shape, dtype in shapes],
        in_specs=in_specs,
        out_specs=[out] * len(shapes),
        scratch_shapes=scratch,
        input_output_aliases=alias,
        compiler_params=pltpu.CompilerParams(vmem_limit_bytes=LIMIT),
        cost_estimate=pl.CostEstimate(flops=flops, bytes_accessed=bytes_accessed, transcendentals=0),
    )


def local(blocks, vectors, col_index, row_ptr, send_list):
    k, unknowns = vectors.shape
    rows = unknowns // B
    stored = blocks.shape[0]
    devices = lax.axis_size("dom") * lax.axis_size("sub")
    ghost = send_list.shape[2]
    slots = send_list.shape[1] * ghost
    many = (stored - SHORT * rows) // (LONG - SHORT)
    sizes = (3, 3, 3, 1, 1)
    send_lines = jnp.transpose(send_list, (0, 2, 1))
    inputs = (send_lines, vectors, row_ptr, col_index, blocks)
    here, plan, send, *outgoing = call(
        gather_kernel,
        "gather",
        [(vectors.shape, BF16), ((1, rounded(rows + 1) + rounded(stored)), jnp.int32), (send_lines.shape, jnp.int32)]
        + [((n, ghost, k, B), BF16) for n in sizes],
        [HBM] * 5,
        scratch=[
            pltpu.SMEM(send_lines.shape, jnp.int32),
            pltpu.VMEM(row_ptr.shape, jnp.int32),
            pltpu.VMEM(col_index.shape, jnp.int32),
            pltpu.SemaphoreType.DMA((5,)),
        ],
    )(*[pltpu.with_memory_space_constraint(a, pltpu.HBM) for a in inputs])
    arrived = exchange(*outgoing)
    (partial_image,) = call(
        local_forward_kernel,
        "local_forward",
        [((rows, k, B), F32)],
        [SMEM, VMEM, VMEM],
        flops=2 * rows * LOCAL * B * B * k,
        bytes_accessed=2 * rows * LOCAL * B * B,
    )(plan, here, blocks)
    image, *returns = call(
        ghost_kernel,
        "ghost",
        [((rows, k, B), BF16)] + [((n, ghost, k, B), F32) for n in sizes],
        [VMEM] * 8,
        scratch=[
            pltpu.VMEM((slots, k, B), BF16),
            pltpu.VMEM((rows, k, B), F32),
            pltpu.VMEM((1, slots, k, B), F32),
            pltpu.SMEM((many + 1,), jnp.int32),
            pltpu.SMEM(plan.shape, jnp.int32),
            pltpu.SemaphoreType.DMA,
        ],
        flops=4 * (stored - rows * LOCAL) * B * B * k,
        bytes_accessed=4 * (stored - rows * LOCAL) * B * B,
    )(plan, blocks, partial_image, *arrived)
    returned = exchange(*returns)
    partial_adjoint, norms = call(
        local_backward_kernel,
        "local_backward",
        [((k, unknowns), F32), ((1, B), F32)],
        [SMEM, VMEM, VMEM],
        flops=2 * rows * LOCAL * B * B * k,
        bytes_accessed=2 * rows * LOCAL * B * B,
    )(plan, blocks, image)
    adjoint, packed = call(
        gram_kernel,
        "gram",
        [((k, unknowns), F32), ((devices, 4, B), F32)],
        [SMEM] + [VMEM] * 7,
        alias={1: 0},
    )(send, partial_adjoint, norms, *returned)
    everywhere = lax.all_to_all(packed, AXES, 0, 0)
    parts = 4
    basis, factor, gain = call(
        functools.partial(solve_kernel, unknowns * devices),
        "solve",
        [((k, unknowns), F32), ((k, k), F32), ((1, k), F32)],
        [VMEM, VMEM],
        scratch=[
            pltpu.VMEM((k, unknowns), F32),
            pltpu.VMEM((k, k), F32),
            pltpu.VMEM((1, k), F32),
            pltpu.SemaphoreType.DMA((parts + 2,)),
        ],
        out=HBM,
    )(everywhere, adjoint)
    return basis, factor, gain[0]


def solution(mesh):
    return jax.shard_map(
        local,
        mesh=mesh,
        in_specs=(
            P(AXES, None, None),
            P(None, AXES),
            P(AXES, None),
            P(AXES, None),
            P(AXES, None, None),
        ),
        out_specs=(P(None, AXES), P(), P()),
        check_vma=False,
    )
```
